256 devices in a mesh: dp: 32 (over y, z_hi, core), tensor: 8 (over z_lo, x).
Axes of the slice: x: 4, y: 4, z: 8 (z_hi: 4, z_lo: 2; z = z_hi * 2 + z_lo), core: 2. Of those that a mesh axis runs over, the one named last changes fastest.
Arguments:
- attended: bfloat16 [8192, 6144], P('dp', 'tensor'), may hold values from -6 to 6
- out_weight: bfloat16 [6144, 6144], P('tensor'), may hold values from -0.078125 to 0.078125
- encoder: bfloat16 [6144, 768], P('tensor'), may hold values from -0.078125 to 0.078125
- decoder: bfloat16 [768, 6144], P(None, 'tensor'), may hold values from -0.21875 to 0.21875
- grad_out: bfloat16 [8192, 6144], P('dp', 'tensor'), may hold values from -6 to 6
Outputs:
- decoded: bfloat16 [8192, 6144], P('dp', 'tensor')
- grad_attended: bfloat16 [8192, 6144], P('dp', 'tensor')
- grad_weight: float32 [6144, 6144], P('tensor', 'dp')
- grad_encoder: float32 [6144, 768], P('tensor', 'dp')
- grad_decoder: float32 [768, 6144], P('dp', 'tensor')
The draws below stay inside these ranges and needn't reach their ends.
All inputs are finite; a program needn't handle non-finite values.
Results may differ from the reference program's by a relative error of at most 0.025.
Values may be sent and summed in bfloat16 or wider, within the bound.
A program may use at most 128 MiB of HBM per device.

```python
import jax
import jax.numpy as jnp
from jax import lax

D = 6144
R = 768
TOK = 256
HD = 6144
TOKENS = 8192
HEAD_GROUPS = 8
DATA_GROUPS = 32


def level_of(stream_key, extent, pieces, low, top_value):
    def one(dim, shards_of):
        steps = jax.random.uniform(jax.random.fold_in(jax.random.fold_in(stream_key, 6), dim), (shards_of,), jnp.float32, low / len(pieces), top_value / len(pieces))
        return jnp.repeat(jnp.exp(steps), extent[dim] // shards_of).reshape((-1,) + (1,) * (len(extent) - dim - 1))

    gain = one(*pieces[0])
    for cut in pieces[1:]:
        gain = gain * one(*cut)
    return gain


def gaussian(own_key, shape, scale, reach, shards=(), kind=jnp.bfloat16):
    loudness = level_of(own_key, shape, shards, -0.22, 0.18) if shards else 1.0
    values = jax.random.normal(own_key, shape, jnp.float32) * scale * loudness
    return jnp.minimum(jnp.maximum(values, -reach), reach).astype(kind)


def setup_inputs(seed: int = 0) -> dict:
    seeds = jax.random.split(jax.random.key(seed), 6)
    attended = gaussian(seeds[0], (TOKENS, HD), 1.0, 6.0, ((0, 32), (1, 8)))
    out_weight = gaussian(seeds[1], (HD, D), HD ** -0.5, 0.078125, ((0, 8),))
    encoder = gaussian(seeds[2], (D, R), D ** -0.5, 0.078125, ((0, 8),))
    decoder = gaussian(seeds[3], (R, D), R ** -0.5, 0.21875, ((1, 8),))
    grad_out = gaussian(seeds[4], (TOKENS, D), 1.0, 6.0, ((0, 32), (1, 8)))
    return {"attended": attended, "out_weight": out_weight, "encoder": encoder, "decoder": decoder, "grad_out": grad_out}


def reference(attended, out_weight, encoder, decoder, grad_out):
    group_width = HD // HEAD_GROUPS
    grad_scale = 1.0 / float(TOKENS) ** 0.5
    encoded = jnp.zeros((TOKENS, R), jnp.float32)
    summed = jnp.zeros((TOKENS, D), jnp.float32)
    for head_group in range(HEAD_GROUPS):
        lower = head_group * group_width
        partial_value = jnp.dot(attended[:, lower:lower + group_width], out_weight[lower:lower + group_width],
                          preferred_element_type=jnp.float32).astype(jnp.bfloat16)
        encoded = encoded + jnp.dot(partial_value, encoder, preferred_element_type=jnp.float32)
        summed = summed + partial_value.astype(jnp.float32)
    code_word = encoded.astype(jnp.bfloat16)
    decoded = jnp.dot(code_word, decoder, preferred_element_type=jnp.float32).astype(jnp.bfloat16)
    grad_code = jnp.dot(grad_out, decoder.T, preferred_element_type=jnp.float32).astype(jnp.bfloat16)
    grad_partial = jnp.dot(grad_code, encoder.T, preferred_element_type=jnp.float32).astype(jnp.bfloat16)
    grad_attended = jnp.dot(grad_partial, out_weight.T, preferred_element_type=jnp.float32).astype(jnp.bfloat16)

    def rounded(value):
        return lax.optimization_barrier((grad_scale * value).astype(jnp.bfloat16)).astype(jnp.float32)

    def accumulate(carry, stacked):
        acc_weight, acc_encoder, acc_decoder = carry
        att_rows, gp_rows, sum_rows, gc_rows, cw_rows, go_rows = stacked
        acc_weight = acc_weight + rounded(jnp.dot(att_rows.T, gp_rows, preferred_element_type=jnp.float32))
        acc_encoder = acc_encoder + rounded(jnp.dot(sum_rows.T, gc_rows.astype(jnp.float32),
                                                    precision=lax.Precision.HIGHEST))
        acc_decoder = acc_decoder + rounded(jnp.dot(cw_rows.T, go_rows, preferred_element_type=jnp.float32))
        return (acc_weight, acc_encoder, acc_decoder), None

    stacked = (attended.reshape(DATA_GROUPS, TOK, HD), grad_partial.reshape(DATA_GROUPS, TOK, D),
               summed.reshape(DATA_GROUPS, TOK, D), grad_code.reshape(DATA_GROUPS, TOK, R),
               code_word.reshape(DATA_GROUPS, TOK, R), grad_out.reshape(DATA_GROUPS, TOK, D))
    start_carry = (jnp.zeros((HD, D), jnp.float32), jnp.zeros((D, R), jnp.float32), jnp.zeros((R, D), jnp.float32))
    (grad_weight, grad_encoder, grad_decoder), unused = lax.scan(accumulate, start_carry, stacked)
    return decoded, grad_attended, grad_weight, grad_encoder, grad_decoder
```

```python
import jax
import jax.numpy as jnp
from jax import lax
from jax.experimental import pallas as pl
from jax.experimental.pallas import tpu as pltpu
from jax.sharding import PartitionSpec as P

MESH = pl.DeviceIdType.MESH
F32 = jnp.float32
BF16 = jnp.bfloat16
TOK = 256
W = 768
H = W // 2
NY, NZ, NT = 4, 4, 8
YB = W // NY
ZB = YB // NZ
CB = ZB // 2
TB = TOK // NT
ER = W // 4
SCALE = 1.0 / float(8192) ** 0.5
N_COPIES = 96


def mm(a, b, ca, cb):
    return lax.dot_general(a, b, (((ca,), (cb,)), ((), ())), preferred_element_type=F32)


def kernel(
    att_h, w_h, enc_h, dec_h, go_h,
    dec_out, ga_out, gw_out, ge_out, gd_out,
    att, wv, enc, dec, go,
    gcs, gcr, gcc, gcf, gct,
    etr, kacc, ksnd, krcv, kt,
    mown, moth, mrcv, mya, myr, myb, myra, myrr, myrb, ms2,
    mza, mzr, mzb, mzra, mzrr, mzrb, mch, mt,
    gs, gr, gsum, gswp, ge_v,
    cws, cwr, cwc, cwf, cwt,
    down, doth, drcv, dya, dyr, dyb, dyra, dyrr, dyrb, ds2,
    dza, dzr, dzb, dzra, dzrr, dzrb, dsum, dswp, gd_v,
    erow, dec_v, ga_v, gw_v,
    lsem, ssem, rsem,
):
    d = lax.axis_index("dp")
    t = lax.axis_index("tensor")
    y, z, c = d // 8, (d // 2) % 4, d % 2
    zl, x = t // 4, t % 4
    sgn = 1 - 2 * c

    def dp_dev(yy, zz, cc):
        return {"dp": ((yy + 4) % 4 * 4 + (zz + 4) % 4) * 2 + cc}

    other = dp_dev(y, z, 1 - c)
    y_next, y_prev = dp_dev(y + sgn, z, c), dp_dev(y - sgn, z, c)
    z_next, z_prev = dp_dev(y, z + sgn, c), dp_dev(y, z - sgn, c)

    def t_to(k):
        kz, kx = k // 4, k % 4
        return (1 - zl if kz else zl) * 4 + (x + kx) % 4

    def t_from(k):
        kz, kx = k // 4, k % 4
        return (1 - zl if kz else zl) * 4 + (x + 4 - kx) % 4

    order = (1, 3, 4, 5, 7, 2, 6)

    def half(cc):
        return pl.ds(pl.multiple_of(cc * H, 128), H)

    def rows(i, n):
        return pl.ds(pl.multiple_of(i * n, n), n)

    me_h, ot_h = half(c), half(1 - c)
    zrow = rows(y * 4 + z, ZB)

    counter = [0]
    sent = []

    def remote(src, dst, dev):
        i = counter[0]
        counter[0] += 1
        cp = pltpu.make_async_remote_copy(
            src_ref=src, dst_ref=dst, send_sem=ssem.at[i], recv_sem=rsem.at[i],
            device_id=dev, device_id_type=MESH,
        )
        return cp

    def send(src, dst, dev):
        cp = remote(src, dst, dev)
        cp.start()
        sent.append(cp)
        return cp

    lcount = [0]

    def local(src, dst):
        i = lcount[0]
        lcount[0] += 1
        cp = pltpu.make_async_copy(src, dst, lsem.at[i])
        cp.start()
        return cp

    l_go = local(go_h, go)
    l_dec = local(dec_h, dec)
    l_enc = local(enc_h, enc)
    l_w = []
    for i in range(NT):
        cols = pl.ds(pl.multiple_of(i * W + c * H, 128), H)
        l_w.append(local(w_h.at[:, cols], wv.at[i]))
    l_att = local(att_h, att)

    barrier = pltpu.get_barrier_semaphore()
    partners = [{"tensor": t_to(k)} for k in order] + [other, y_next, y_prev, z_next, z_prev]
    for dev in partners:
        pl.semaphore_signal(barrier, inc=1, device_id=dev, device_id_type=MESH)

    l_enc.wait()
    pick = (
        lax.broadcasted_iota(jnp.int32, (ZB, W), 1)
        == lax.broadcasted_iota(jnp.int32, (ZB, W), 0) + (y * 4 + z) * ZB
    )
    pick = jnp.where(pick, 1.0, 0.0).astype(BF16)
    etr[0] = mm(pick, enc[rows(c, H), :], 1, 1).astype(BF16)
    l_go.wait()
    l_dec.wait()
    gcs[...] = mm(go[...], dec[...], 1, 1).astype(BF16)

    pl.semaphore_wait(barrier, len(partners))

    et_in = {k: send(etr.at[0], etr.at[k], {"tensor": t_to(k)}) for k in order}
    gc_in = {
        k: send(gcs.at[rows(t_to(k), TB), :], gcr.at[k], {"tensor": t_to(k)}) for k in order
    }

    t_own = d // 4
    rx, rz = (x + 4 - t_own % 4) % 4, (zl + t_own // 4) % 2
    is_own = jnp.logical_and(rx == 0, rz == 0)
    is_two = jnp.logical_and(rx == 0, rz == 1)
    is_three = rx % 2 == 1
    is_last = rx == 2
    passes_on = rx == 1 + 2 * c
    e_recv = counter[0]
    counter[0] += 1
    e_send = [counter[0] + i for i in range(4)]
    counter[0] += 4

    def e_copy(i, dev):
        return pltpu.make_async_remote_copy(
            src_ref=erow, dst_ref=erow, send_sem=ssem.at[e_send[i]], recv_sem=rsem.at[e_recv],
            device_id={"tensor": dev}, device_id_type=MESH,
        )

    e_z = e_copy(0, (1 - zl) * 4 + x)
    e_p = e_copy(1, zl * 4 + (x + 1) % 4)
    e_m = e_copy(2, zl * 4 + (x + 3) % 4)
    e_f = e_copy(3, zl * 4 + (x + 4 + sgn) % 4)

    @pl.when(is_own)
    def _():
        erow[...] = enc[rows(d % 4, ER), :]
        e_z.start()
        e_p.start()
        e_m.start()

    total = None
    for k in (0,) + order:
        if k:
            et_in[k].wait_recv()
        else:
            for cp in l_w:
                cp.wait()
        term = mm(etr[k], wv[t_from(k)], 1, 1)
        total = term if total is None else total + term
    kacc[...] = total
    ksnd[...] = kacc[:, ot_h].astype(BF16)
    k_core = send(ksnd, krcv, other)

    def chunk_sum(own, recv, copies):
        acc = own[rows(t, TB), :].astype(F32)
        for k in order:
            copies[k].wait_recv()
            acc = acc + recv[k].astype(F32)
        return acc.astype(BF16)

    gcc[...] = chunk_sum(gcs, gcr, gc_in)
    gcf[rows(t, TB), :] = gcc[...]
    gcf_in = {k: send(gcc, gcf.at[rows(t, TB), :], {"tensor": t_to(k)}) for k in order}

    def gather_start(buf, row0, n, nxt, prv):
        blk = buf.at[row0, me_h]
        a = send(blk, blk, nxt)
        b = send(blk, blk, prv)
        return a, b

    def z_rows(zz):
        return rows(y * 4 + (zz + 4) % 4, ZB)

    def y_rows(yy):
        return rows((yy + 4) % 4, YB)

    k_core.wait_recv()
    kt[zrow, me_h] = (kacc[:, me_h] + krcv[...].astype(F32)).astype(BF16)

    class Gather:
        def __init__(self, buf):
            self.buf = buf
            self.core_in = []

        def push(self, r, dev):
            blk = self.buf.at[r, me_h]
            return send(blk, blk, dev)

        def core(self, r):
            self.core_in.append(self.push(r, other))

        def z_start(self):
            self.a, self.b = self.push(zrow, z_next), self.push(zrow, z_prev)

        def z_mid(self):
            self.a.wait_recv()
            self.f = self.push(z_rows(z - sgn), z_next)

        def z_end(self):
            self.b.wait_recv()
            self.f.wait_recv()

        def y_start(self):
            self.a, self.b = self.push(y_rows(y), y_next), self.push(y_rows(y), y_prev)
            self.core(y_rows(y))

        def y_mid(self):
            self.a.wait_recv()
            self.f = self.push(y_rows(y - sgn), y_next)
            self.core(y_rows(y - sgn))

        def y_end(self):
            self.b.wait_recv()
            self.core(y_rows(y + sgn))
            self.f.wait_recv()
            self.core(y_rows(y + 2 * sgn))

        def finish(self):
            for cp in self.core_in:
                cp.wait_recv()

    kg = Gather(kt)
    kg.z_start()

    class Scatter:
        def __init__(self, lhs_t, right, own, oth, rcv, ya, yr, yb, yra, yrr, yrb, s2, za, zr, zb, zra, zrr, zrb):
            self.lhs_t, self.right, self.own, self.oth, self.rcv = lhs_t, right, own, oth, rcv
            self.yst = (ya, yr, yb, yra, yrr, yrb)
            self.zst = (za, zr, zb, zra, zrr, zrb)
            self.s2 = s2

        def core_start(self):
            for i in range(3):
                r = slice(i * 256, (i + 1) * 256)
                self.oth[r, :] = mm(self.lhs_t[r, :], self.right[:, ot_h], 1, 0).astype(BF16)
            self.cp = send(self.oth, self.rcv, other)
            for i in range(3):
                r = slice(i * 256, (i + 1) * 256)
                self.own[r, :] = mm(self.lhs_t[r, :], self.right[:, me_h], 1, 0)

        def y_term(self, yy):
            r = y_rows(yy)
            return self.own[r, :] + self.rcv[r, :].astype(F32)

        def z_term(self, zz):
            return self.s2[rows((zz + 4) % 4, ZB), :]

        def ring_start(self, term, pos, bufs, nxt, prv):
            a, r, b, ra, rr, rb = bufs
            r[...] = term(pos + 2 * sgn).astype(BF16)
            self.r_in = send(r, rr, nxt)
            a[...] = term(pos - sgn).astype(BF16)
            self.a_in = send(a, ra, prv)

        def ring_mid(self, term, pos, bufs, nxt):
            a, r, b, ra, rr, rb = bufs
            self.r_in.wait_recv()
            b[...] = (term(pos + sgn) + rr[...].astype(F32)).astype(BF16)
            self.b_in = send(b, rb, nxt)

        def ring_end(self, term, pos, bufs):
            a, r, b, ra, rr, rb = bufs
            self.a_in.wait_recv()
            own = term(pos) + ra[...].astype(F32)
            self.b_in.wait_recv()
            return own + rb[...].astype(F32)

        def y_start(self):
            self.cp.wait_recv()
            self.ring_start(self.y_term, y, self.yst, y_next, y_prev)

        def y_mid(self):
            self.ring_mid(self.y_term, y, self.yst, y_next)

        def y_end(self):
            self.s2[...] = self.ring_end(self.y_term, y, self.yst)

        def z_start(self):
            self.ring_start(self.z_term, z, self.zst, z_next, z_prev)

        def z_mid(self):
            self.ring_mid(self.z_term, z, self.zst, z_next)

        def z_end(self):
            return self.ring_end(self.z_term, z, self.zst)

    for k in order:
        gcf_in[k].wait_recv()
    gct[...] = gcf[...].T
    l_att.wait()
    ms = Scatter(gct, att, mown, moth, mrcv, mya, myr, myb, myra, myrr, myrb, ms2, mza, mzr, mzb, mzra, mzrr, mzrb)
    ms.core_start()

    kg.z_mid()
    kg.z_end()
    kg.y_start()
    ms.y_start()

    @pl.when(is_two)
    def _():
        e_z.wait_recv()
        e_p.start()
        e_m.start()

    kg.y_mid()
    ms.y_mid()
    kg.y_end()

    @pl.when(is_three)
    def _():
        e_z.wait_recv()

    @pl.when(passes_on)
    def _():
        e_f.start()

    kg.finish()

    cws[...] = mm(att[...], kt[...], 1, 1).astype(BF16)
    cw_in = {
        k: send(cws.at[rows(t_to(k), TB), :], cwr.at[k], {"tensor": t_to(k)}) for k in order
    }
    ms.y_end()
    ms.z_start()
    ga_v[...] = mm(gcf[...], kt[...], 1, 0).astype(BF16)
    o_ga = local(ga_v, ga_out)
    ms.z_mid()
    cwc[...] = chunk_sum(cws, cwr, cw_in)
    cwf[rows(t, TB), :] = cwc[...]
    cwf_in = {k: send(cwc, cwf.at[rows(t, TB), :], {"tensor": t_to(k)}) for k in order}

    m_block = ms.z_end().astype(BF16)
    mt[zrow, me_h] = m_block
    mch[c] = m_block
    m_core = send(mch.at[c], mch.at[c], other)
    mg = Gather(mt)
    mg.z_start()

    for k in order:
        cwf_in[k].wait_recv()
    cwt[...] = cwf[...].T
    ds = Scatter(cwt, go, down, doth, drcv, dya, dyr, dyb, dyra, dyrr, dyrb, ds2, dza, dzr, dzb, dzra, dzrr, dzrb)
    ds.core_start()

    mg.z_mid()
    mg.z_end()
    mg.y_start()
    ds.y_start()

    m_core.wait_recv()
    g_in = {}
    for k in order + (0,):
        val = mm(mch[0], wv[t_to(k), :H, :], 1, 0) + mm(mch[1], wv[t_to(k), H:, :], 1, 0)
        if k:
            gs[k] = val.astype(BF16)
            g_in[k] = send(gs.at[k], gr.at[k], {"tensor": t_to(k)})
        else:
            gsum[...] = val

    mg.y_mid()
    ds.y_mid()
    dec_v[...] = mm(cwf[...], dec[...], 1, 0).astype(BF16)
    o_dec = local(dec_v, dec_out)
    mg.y_end()

    for k in order:
        g_in[k].wait_recv()
        gsum[...] += gr[k].astype(F32)
    g_core = send(gsum.at[rows(1 - c, CB), :], gswp, other)

    ds.y_end()
    ds.z_start()

    @pl.when(is_last)
    def _():
        e_z.wait_recv()

    mg.finish()
    gw_v[...] = (SCALE * mm(erow[...], mt[...], 1, 0)).T
    o_gw = local(gw_v, gw_out)

    ds.z_mid()
    g_core.wait_recv()
    ge_v[me_h, :] = (SCALE * gsum[rows(c, CB), :]).T
    ge_v[ot_h, :] = (SCALE * gswp[...]).T
    o_ge = local(ge_v, ge_out)

    dsum[...] = ds.z_end()
    d_core = send(dsum.at[rows(1 - c, CB), :], dswp, other)
    gd_v[:, me_h] = SCALE * dsum[rows(c, CB), :]
    d_core.wait_recv()
    gd_v[:, ot_h] = SCALE * dswp[...]
    o_gd = local(gd_v, gd_out)

    for cp in sent:
        cp.wait_send()

    @pl.when(is_own)
    def _():
        e_z.wait_send()

    @pl.when(rx == 0)
    def _():
        e_p.wait_send()
        e_m.wait_send()

    @pl.when(passes_on)
    def _():
        e_f.wait_send()

    for cp in (o_ga, o_dec, o_gw, o_ge, o_gd):
        cp.wait()
    assert counter[0] <= N_COPIES, counter


def ring_scratch(n):
    return [pltpu.VMEM((n, H), BF16)] * 6


def scatter_scratch():
    return (
        [pltpu.VMEM((W, H), F32), pltpu.VMEM((W, H), BF16), pltpu.VMEM((W, H), BF16)]
        + ring_scratch(YB)
        + [pltpu.VMEM((YB, H), F32)]
        + ring_scratch(ZB)
    )


def body(attended, out_weight, encoder, decoder, grad_out):
    v = pltpu.VMEM
    scratch = (
        [v((TOK, W), BF16), v((NT, W, H), BF16), v((W, W), BF16), v((W, W), BF16), v((TOK, W), BF16)]
        + [v((TOK, W), BF16), v((NT, TB, W), BF16), v((TB, W), BF16), v((TOK, W), BF16), v((W, TOK), BF16)]
        + [v((NT, ZB, H), BF16), v((ZB, W), F32), v((ZB, H), BF16), v((ZB, H), BF16), v((W, W), BF16)]
        + scatter_scratch()
        + [v((2, ZB, H), BF16), v((W, W), BF16)]
        + [v((NT, ZB, H), BF16), v((NT, ZB, H), BF16), v((ZB, H), F32), v((CB, H), F32), v((W, CB), F32)]
        + [v((TOK, W), BF16), v((NT, TB, W), BF16), v((TB, W), BF16), v((TOK, W), BF16), v((W, TOK), BF16)]
        + scatter_scratch()
        + [v((ZB, H), F32), v((CB, H), F32), v((CB, W), F32)]
        + [v((ER, W), BF16), v((TOK, W), BF16), v((TOK, W), BF16), v((W, ER), F32)]
        + [
            pltpu.SemaphoreType.DMA((20,)),
            pltpu.SemaphoreType.DMA((N_COPIES,)),
            pltpu.SemaphoreType.DMA((N_COPIES,)),
        ]
    )
    hbm = pl.BlockSpec(memory_space=pl.ANY)
    return pl.pallas_call(
        kernel,
        out_shape=(
            jax.ShapeDtypeStruct((TOK, W), BF16),
            jax.ShapeDtypeStruct((TOK, W), BF16),
            jax.ShapeDtypeStruct((W, ER), F32),
            jax.ShapeDtypeStruct((W, CB), F32),
            jax.ShapeDtypeStruct((CB, W), F32),
        ),
        in_specs=[hbm] * 5,
        out_specs=[hbm] * 5,
        scratch_shapes=scratch,
        compiler_params=pltpu.CompilerParams(
            collective_id=0, has_side_effects=True, vmem_limit_bytes=48 * 1024 * 1024
        ),
    )(attended, out_weight, encoder, decoder, grad_out)


def solution(mesh):
    return jax.shard_map(
        body,
        mesh=mesh,
        in_specs=(
            P("dp", "tensor"),
            P("tensor", None),
            P("tensor", None),
            P(None, "tensor"),
            P("dp", "tensor"),
        ),
        out_specs=(
            P("dp", "tensor"),
            P("dp", "tensor"),
            P("tensor", "dp"),
            P("tensor", "dp"),
            P("dp", "tensor"),
        ),
        check_vma=False,
    )
```

```python
import jax
import jax.numpy as jnp
from jax import lax
from jax.experimental import pallas as pl
from jax.experimental.pallas import tpu as pltpu
from jax.sharding import PartitionSpec as P

MESH = pl.DeviceIdType.MESH
F32 = jnp.float32
BF16 = jnp.bfloat16
TOK = 256
W = 768
H = W // 2
NY, NZ, NT = 4, 4, 8
YB = W // NY
ZB = YB // NZ
CB = ZB // 2
TB = TOK // NT
ER = W // 4
SCALE = 1.0 / float(8192) ** 0.5
N_COPIES = 140
VMEM_LIMIT = 62 * 1024 * 1024


def mm(a, b, ca, cb):
    return lax.dot_general(a, b, (((ca,), (cb,)), ((), ())), preferred_element_type=F32)


def kernel(
    att_h, w_h, enc_h, dec_h, go_h,
    dec_out, ga_out, gw_out, ge_out, gd_out,
    att, wv, enc, dec, go,
    gcs, gcr, gcc, gcf, gct,
    etr, kacc, ksnd, krcv, kt,
    m0, m1, m2, m3, m4, m5, m6, m7, mch, mt,
    gs, gr, gsum, gswp, ge_v,
    cws, cwr, cwc, cwf, cwt,
    d0, d1, d2, d3, d4, d5, d6, d7, dsum, dswp, gd_v,
    erow, dec_v, ga_v, gw_v,
    lsem, ssem, rsem,
):
    d = lax.axis_index("dp")
    t = lax.axis_index("tensor")
    y, z, c = d // 8, (d // 2) % 4, d % 2
    zl, x = t // 4, t % 4
    sgn = 1 - 2 * c

    def dp_dev(yy, zz, cc):
        return {"dp": (yy % 4 * 4 + zz % 4) * 2 + cc}

    other = dp_dev(y, z, 1 - c)

    def y_dev(j):
        return dp_dev(y + j, z, c)

    def z_dev(k):
        return dp_dev(y, z + k, c)

    def t_to(k):
        kz, kx = k // 4, k % 4
        return (1 - zl if kz else zl) * 4 + (x + kx) % 4

    def t_from(k):
        kz, kx = k // 4, k % 4
        return (1 - zl if kz else zl) * 4 + (x + 4 - kx) % 4

    order = (2, 6, 5, 7, 1, 3, 4)
    arrive = (1, 3, 4, 5, 7, 2, 6)

    def half(cc):
        return pl.ds(pl.multiple_of(cc * H, 128), H)

    def rows(i, n):
        return pl.ds(pl.multiple_of(i * n, n), n)

    me_h, ot_h = half(c), half(1 - c)

    def y_rows(yy):
        return rows((yy + 4) % 4, YB)

    def yz_rows(yy, zz):
        return rows((yy + 4) % 4 * 4 + (zz + 4) % 4, ZB)

    counter = [0]
    sent = []

    def remote(src, dst, dev):
        i = counter[0]
        counter[0] += 1
        cp = pltpu.make_async_remote_copy(
            src_ref=src, dst_ref=dst, send_sem=ssem.at[i], recv_sem=rsem.at[i],
            device_id=dev, device_id_type=MESH,
        )
        return cp

    def send(src, dst, dev):
        cp = remote(src, dst, dev)
        cp.start()
        sent.append(cp)
        return cp

    lcount = [0]

    def local(src, dst):
        i = lcount[0]
        lcount[0] += 1
        cp = pltpu.make_async_copy(src, dst, lsem.at[i])
        cp.start()
        return cp

    barrier = pltpu.get_barrier_semaphore()
    partners = (
        [{"tensor": t_to(k)} for k in order]
        + [y_dev(j) for j in (2, 1, 3)]
        + [z_dev(k) for k in (2, 1, 3)]
        + [other]
    )
    for dev in partners:
        pl.semaphore_signal(barrier, inc=1, device_id=dev, device_id_type=MESH)
    l_enc = local(enc_h, enc)
    l_go = local(go_h, go)
    l_dec = local(dec_h, dec)
    l_w = []
    for i in range(NT):
        cols = pl.ds(pl.multiple_of(i * W + c * H, 128), H)
        l_w.append(local(w_h.at[:, cols], wv.at[i]))
    l_att = local(att_h, att)

    l_enc.wait()
    pick = (
        lax.broadcasted_iota(jnp.int32, (ZB, W), 1)
        == lax.broadcasted_iota(jnp.int32, (ZB, W), 0) + (y * 4 + z) * ZB
    )
    pick = jnp.where(pick, 1.0, 0.0).astype(BF16)
    etr[0] = mm(pick, enc[rows(c, H), :], 1, 1).astype(BF16)
    l_go.wait()
    l_dec.wait()
    gcs[...] = mm(go[...], dec[...], 1, 1).astype(BF16)

    pl.semaphore_wait(barrier, len(partners))

    et_in = {k: send(etr.at[0], etr.at[k], {"tensor": t_to(k)}) for k in order}
    gc_in = {
        k: send(gcs.at[rows(t_to(k), TB), :], gcr.at[k], {"tensor": t_to(k)}) for k in order
    }

    t_own = d // 4
    rx, rz = (x + 4 - t_own % 4) % 4, (zl + t_own // 4) % 2
    is_own = jnp.logical_and(rx == 0, rz == 0)
    is_two = jnp.logical_and(rx == 0, rz == 1)
    is_three = rx % 2 == 1
    is_last = rx == 2
    passes_on = rx == 1 + 2 * c
    e_recv = counter[0]
    counter[0] += 1
    e_send = [counter[0] + i for i in range(4)]
    counter[0] += 4

    def e_copy(i, dev):
        return pltpu.make_async_remote_copy(
            src_ref=erow, dst_ref=erow, send_sem=ssem.at[e_send[i]], recv_sem=rsem.at[e_recv],
            device_id={"tensor": dev}, device_id_type=MESH,
        )

    class Tree:
        def __init__(self):
            self.z = e_copy(0, (1 - zl) * 4 + x)
            self.p = e_copy(1, zl * 4 + (x + 1) % 4)
            self.m = e_copy(2, zl * 4 + (x + 3) % 4)
            self.f = e_copy(3, zl * 4 + (x + 4 + sgn) % 4)
            self.at = 0

        def step(self):
            self.at += 1
            if self.at == 1:

                @pl.when(is_own)
                def _():
                    erow[...] = enc[rows(d % 4, ER), :]
                    self.z.start()
                    self.p.start()
                    self.m.start()

            elif self.at == 2:

                @pl.when(is_two)
                def _():
                    self.z.wait_recv()
                    self.p.start()
                    self.m.start()

            elif self.at == 3:

                @pl.when(is_three)
                def _():
                    self.z.wait_recv()

                @pl.when(passes_on)
                def _():
                    self.f.start()

            elif self.at == 4:

                @pl.when(is_last)
                def _():
                    self.z.wait_recv()

        def drain(self):
            if self.at == 0:
                return
            while self.at < 4:
                self.step()

            @pl.when(is_own)
            def _():
                self.z.wait_send()

            @pl.when(rx == 0)
            def _():
                self.p.wait_send()
                self.m.wait_send()

            @pl.when(passes_on)
            def _():
                self.f.wait_send()

    tree = Tree()

    total = None
    for k in (0,) + arrive:
        if k:
            et_in[k].wait_recv()
        else:
            for cp in l_w:
                cp.wait()
        term = mm(etr[k], wv[t_from(k)], 1, 1)
        total = term if total is None else total + term
    kacc[...] = total
    ksnd[...] = kacc[:, ot_h].astype(BF16)
    k_core = send(ksnd, krcv, other)

    def chunk_sum(own, recv, copies):
        acc = own[rows(t, TB), :].astype(F32)
        for k in arrive:
            copies[k].wait_recv()
            acc = acc + recv[k].astype(F32)
        return acc.astype(BF16)

    gcc[...] = chunk_sum(gcs, gcr, gc_in)
    gcf[rows(t, TB), :] = gcc[...]
    gcf_in = {k: send(gcc, gcf.at[rows(t, TB), :], {"tensor": t_to(k)}) for k in order}

    class Gather:
        def __init__(self, buf):
            self.buf = buf
            self.yc = {}
            self.cc = []

        def push(self, r, dev):
            blk = self.buf.at[r, me_h]
            return send(blk, blk, dev)

        def y_send(self, k):
            for j in (2, 1, 3):
                self.yc[k, j] = self.push(yz_rows(y, z - k), y_dev(j))

        def start(self):
            self.zc = {k: self.push(yz_rows(y, z), z_dev(k)) for k in (2, 1, 3)}
            self.y_send(0)

        def z_step(self, k):
            self.zc[k].wait_recv()
            self.y_send(k)

        def z_rest(self):
            for k in (1, 3, 2):
                self.z_step(k)
            self.cc.append(self.push(y_rows(y), other))

        def y_step(self, j):
            for k in (0, 1, 3, 2):
                self.yc[k, j].wait_recv()
            self.cc.append(self.push(y_rows(y - j), other))

        def y_rest(self):
            for j in (1, 3, 2):
                self.y_step(j)

        def finish(self):
            for cp in self.cc:
                cp.wait_recv()

    class Scatter:
        def __init__(self, lhs_t, right, bufs):
            self.lhs_t, self.right = lhs_t, right
            self.own, self.oth, self.rcv, self.ys, self.yr, self.zs, self.zr, self.zown = bufs

        def core_start(self):
            self.cc = {}
            for j in (2, 1, 3, 0):
                r = y_rows(y + j)
                self.oth[r, :] = mm(self.lhs_t[r, :], self.right[:, ot_h], 1, 0).astype(BF16)
                self.cc[j] = send(self.oth.at[r, :], self.rcv.at[r, :], other)
            for j in (2, 1, 3, 0):
                r = y_rows(y + j)
                self.own[r, :] = mm(self.lhs_t[r, :], self.right[:, me_h], 1, 0)

        def y_start(self):
            self.yc = {}
            for j in (2, 1, 3):
                r = y_rows(y + j)
                self.cc[j].wait_recv()
                self.ys[j - 1] = (self.own[r, :] + self.rcv[r, :].astype(F32)).astype(BF16)
            for k in (2, 1, 3, 0):
                r = rows((z + k) % 4, ZB)
                for j in (2, 1, 3):
                    self.yc[k, j] = send(self.ys.at[j - 1, r, :], self.yr.at[j - 1, r, :], y_dev(j))
            self.cc[0].wait_recv()

        def z_start(self):
            self.zc = {}
            for k in (2, 1, 3, 0):
                r = rows((z + k) % 4, ZB)
                yz = yz_rows(y, z + k)
                val = self.own[yz, :] + self.rcv[yz, :].astype(F32)
                for j in (1, 3, 2):
                    self.yc[k, j].wait_recv()
                    val = val + self.yr[j - 1, r, :].astype(F32)
                if k:
                    self.zs[k - 1] = val.astype(BF16)
                    self.zc[k] = send(self.zs.at[k - 1], self.zr.at[k - 1], z_dev(k))
                else:
                    self.zown[...] = val

        def z_end(self):
            val = self.zown[...]
            for k in (1, 3, 2):
                self.zc[k].wait_recv()
                val = val + self.zr[k - 1].astype(F32)
            return val

    k_core.wait_recv()
    kt[yz_rows(y, z), me_h] = (kacc[:, me_h] + krcv[...].astype(F32)).astype(BF16)
    kg = Gather(kt)
    kg.start()
    kg.z_rest()

    for k in arrive:
        gcf_in[k].wait_recv()
    gct[...] = gcf[...].T
    l_att.wait()
    ms = Scatter(gct, att, (m0, m1, m2, m3, m4, m5, m6, m7))
    ms.core_start()
    ms.y_start()
    tree.step()
    kg.y_rest()
    kg.finish()

    cws[...] = mm(att[...], kt[...], 1, 1).astype(BF16)
    cw_in = {
        k: send(cws.at[rows(t_to(k), TB), :], cwr.at[k], {"tensor": t_to(k)}) for k in order
    }
    ga_v[...] = mm(gcf[...], kt[...], 1, 0).astype(BF16)
    o_ga = local(ga_v, ga_out)
    ms.z_start()
    tree.step()
    cwc[...] = chunk_sum(cws, cwr, cw_in)
    cwf[rows(t, TB), :] = cwc[...]
    cwf_in = {k: send(cwc, cwf.at[rows(t, TB), :], {"tensor": t_to(k)}) for k in order}

    m_block = ms.z_end().astype(BF16)
    mt[yz_rows(y, z), me_h] = m_block
    mch[c] = m_block
    m_core = send(mch.at[c], mch.at[c], other)
    mg = Gather(mt)
    mg.start()

    m_core.wait_recv()
    g_in = {}
    for k in order + (0,):
        val = mm(mch[0], wv[t_to(k), :H, :], 1, 0) + mm(mch[1], wv[t_to(k), H:, :], 1, 0)
        if k:
            gs[k] = val.astype(BF16)
            g_in[k] = send(gs.at[k], gr.at[k], {"tensor": t_to(k)})
        else:
            gsum[...] = val

    tree.step()
    mg.z_rest()
    for k in arrive:
        cwf_in[k].wait_recv()
    cwt[...] = cwf[...].T
    ds = Scatter(cwt, go, (d0, d1, d2, d3, d4, d5, d6, d7))
    ds.core_start()
    ds.y_start()
    dec_v[...] = mm(cwf[...], dec[...], 1, 0).astype(BF16)
    o_dec = local(dec_v, dec_out)
    mg.y_rest()
    for k in arrive:
        g_in[k].wait_recv()
        gsum[...] += gr[k].astype(F32)
    g_core = send(gsum.at[rows(1 - c, CB), :], gswp, other)
    mg.finish()
    tree.step()
    gw_v[...] = SCALE * mm(erow[...], mt[...], 1, 0)
    o_gw = local(gw_v, gw_out)
    g_core.wait_recv()
    ge_v[:, me_h] = SCALE * gsum[rows(c, CB), :]
    ge_v[:, ot_h] = SCALE * gswp[...]
    o_ge = local(ge_v, ge_out)

    ds.z_start()
    dsum[...] = ds.z_end()
    d_core = send(dsum.at[rows(1 - c, CB), :], dswp, other)
    gd_v[:, me_h] = SCALE * dsum[rows(c, CB), :]
    d_core.wait_recv()
    gd_v[:, ot_h] = SCALE * dswp[...]
    o_gd = local(gd_v, gd_out)

    for cp in sent:
        cp.wait_send()
    tree.drain()
    for cp in (o_ga, o_dec, o_gw, o_ge, o_gd):
        cp.wait()
    assert counter[0] <= N_COPIES, counter


def hand_on(*refs):
    ins, outs, held, sem_in, sem_out = refs[:5], refs[5:10], refs[10:15], refs[15], refs[16]
    first = [pltpu.make_async_copy(ins[i], held[i], sem_in.at[i]) for i in range(5)]
    second = [pltpu.make_async_copy(held[i], outs[i], sem_out.at[i]) for i in range(5)]
    for cp in first:
        cp.start()
    for i in (3, 4, 0, 1, 2):
        first[i].wait()
        second[i].start()
    for cp in second:
        cp.wait()


def scatter_scratch():
    v = pltpu.VMEM
    return [
        v((W, H), F32), v((W, H), BF16), v((W, H), BF16), v((3, YB, H), BF16), v((3, YB, H), BF16),
        v((3, ZB, H), BF16), v((3, ZB, H), BF16), v((ZB, H), F32),
    ]


def body(attended, out_weight, encoder, decoder, grad_out):
    v = pltpu.VMEM
    scratch = (
        [v((TOK, W), BF16), v((NT, W, H), BF16), v((W, W), BF16), v((W, W), BF16), v((TOK, W), BF16)]
        + [v((TOK, W), BF16), v((NT, TB, W), BF16), v((TB, W), BF16), v((TOK, W), BF16), v((W, TOK), BF16)]
        + [v((NT, ZB, H), BF16), v((ZB, W), F32), v((ZB, H), BF16), v((ZB, H), BF16), v((W, W), BF16)]
        + scatter_scratch()
        + [v((2, ZB, H), BF16), v((W, W), BF16)]
        + [v((NT, ZB, H), BF16), v((NT, ZB, H), BF16), v((ZB, H), F32), v((CB, H), F32), v((CB, W), F32)]
        + [v((TOK, W), BF16), v((NT, TB, W), BF16), v((TB, W), BF16), v((TOK, W), BF16), v((W, TOK), BF16)]
        + scatter_scratch()
        + [v((ZB, H), F32), v((CB, H), F32), v((CB, W), F32)]
        + [v((ER, W), BF16), v((TOK, W), BF16), v((TOK, W), BF16), v((ER, W), F32)]
        + [
            pltpu.SemaphoreType.DMA((20,)),
            pltpu.SemaphoreType.DMA((N_COPIES,)),
            pltpu.SemaphoreType.DMA((N_COPIES,)),
        ]
    )
    hbm = pl.BlockSpec(memory_space=pl.ANY)
    shapes = (
        jax.ShapeDtypeStruct((TOK, W), BF16),
        jax.ShapeDtypeStruct((TOK, W), BF16),
        jax.ShapeDtypeStruct((ER, W), F32),
        jax.ShapeDtypeStruct((CB, W), F32),
        jax.ShapeDtypeStruct((CB, W), F32),
    )
    results = pl.pallas_call(
        kernel,
        out_shape=shapes,
        in_specs=[hbm] * 5,
        out_specs=[hbm] * 5,
        scratch_shapes=scratch,
        compiler_params=pltpu.CompilerParams(
            collective_id=0, has_side_effects=True, vmem_limit_bytes=VMEM_LIMIT
        ),
    )(attended, out_weight, encoder, decoder, grad_out)
    decoded, grad_attended, weight_t, encoder_t, grad_decoder = pl.pallas_call(
        hand_on,
        out_shape=shapes,
        in_specs=[hbm] * 5,
        out_specs=[hbm] * 5,
        scratch_shapes=[v(a.shape, a.dtype) for a in shapes]
        + [pltpu.SemaphoreType.DMA((5,))] * 2,
        compiler_params=pltpu.CompilerParams(vmem_limit_bytes=VMEM_LIMIT),
    )(*results)
    return decoded, grad_attended, weight_t.T, encoder_t.T, grad_decoder


def solution(mesh):
    return jax.shard_map(
        body,
        mesh=mesh,
        in_specs=(
            P("dp", "tensor"),
            P("tensor", None),
            P("tensor", None),
            P(None, "tensor"),
            P("dp", "tensor"),
        ),
        out_specs=(
            P("dp", "tensor"),
            P("dp", "tensor"),
            P("tensor", "dp"),
            P("tensor", "dp"),
            P("dp", "tensor"),
        ),
        check_vma=False,
    )
```

```python
import jax
import jax.numpy as jnp
from jax import lax
from jax.experimental import pallas as pl
from jax.experimental.pallas import tpu as pltpu
from jax.sharding import PartitionSpec as P

MESH = pl.DeviceIdType.MESH
F32 = jnp.float32
BF16 = jnp.bfloat16
TOK = 256
W = 768
H = W // 2
NY, NZ, NT = 4, 4, 8
YB = W // NY
ZB = YB // NZ
CB = ZB // 2
TB = TOK // NT
ER = W // 4
SCALE = 1.0 / float(8192) ** 0.5
N_COPIES = 140
VMEM_LIMIT = 62 * 1024 * 1024
T1 = 7
T2 = 2
T3 = 3
NO_TREE = False
TG = True
SORD = True
GCPOS = 2
MYP = 1
MZP = 1
MGP = 1


def mm(a, b, ca, cb):
    return lax.dot_general(a, b, (((ca,), (cb,)), ((), ())), preferred_element_type=F32)


def kernel(
    att_h, w_h, enc_h, dec_h, go_h,
    dec_out, ga_out, gw_out, ge_out, gd_out,
    att, wv, enc, dec, go,
    gcs, gcr, gcf, gct,
    etr, kacc, ksnd, krcv, kt,
    m0, m1, m2, m3, m4, m5, m6, m7, mch, mt,
    gs, gr, gsum, gswp, ge_v,
    cws, cwr, cwf, cwt,
    d0, d1, d2, d3, d4, d5, d6, d7, dsum, dswp, gd_v,
    erow, dec_v, ga_v, gw_v,
    lsem, ssem, rsem,
):
    d = lax.axis_index("dp")
    t = lax.axis_index("tensor")
    y, z, c = d // 8, (d // 2) % 4, d % 2
    zl, x = t // 4, t % 4
    sgn = 1 - 2 * c

    def dp_dev(yy, zz, cc):
        return {"dp": (yy % 4 * 4 + zz % 4) * 2 + cc}

    other = dp_dev(y, z, 1 - c)

    def y_dev(j):
        return dp_dev(y + j + 4, z, c)

    def z_dev(k):
        return dp_dev(y, z + k, c)

    def t_to(k):
        kz, kx = k // 4, k % 4
        return (1 - zl if kz else zl) * 4 + (x + kx) % 4

    def t_from(k):
        kz, kx = k // 4, k % 4
        return (1 - zl if kz else zl) * 4 + (x + 4 - kx) % 4

    order = (2, 6, 5, 7, 1, 3, 4)
    arrive = (1, 3, 4, 5, 7, 2, 6)

    def half(cc):
        return pl.ds(pl.multiple_of(cc * H, 128), H)

    def rows(i, n):
        return pl.ds(pl.multiple_of(i * n, n), n)

    me_h, ot_h = half(c), half(1 - c)

    def y_rows(yy):
        return rows((yy + 8) % 4, YB)

    def yz_rows(yy, zz):
        return rows((yy + 8) % 4 * 4 + (zz + 8) % 4, ZB)

    counter = [0]
    sent = []

    def remote(src, dst, dev):
        i = counter[0]
        counter[0] += 1
        cp = pltpu.make_async_remote_copy(
            src_ref=src, dst_ref=dst, send_sem=ssem.at[i], recv_sem=rsem.at[i],
            device_id=dev, device_id_type=MESH,
        )
        return cp

    def send(src, dst, dev):
        cp = remote(src, dst, dev)
        cp.start()
        sent.append(cp)
        return cp

    lcount = [0]

    def local(src, dst):
        i = lcount[0]
        lcount[0] += 1
        cp = pltpu.make_async_copy(src, dst, lsem.at[i])
        cp.start()
        return cp

    barrier = pltpu.get_barrier_semaphore()
    partners = (
        [{"tensor": t_to(k)} for k in order]
        + [y_dev(j) for j in (2, 1, 3)]
        + [z_dev(k) for k in (2, 1, 3)]
        + [other]
    )
    for dev in partners:
        pl.semaphore_signal(barrier, inc=1, device_id=dev, device_id_type=MESH)
    l_enc = local(enc_h.at[rows(c, H), :], enc)
    l_go = local(go_h, go)
    l_dec = local(dec_h, dec)

    l_enc.wait()
    pick = (
        lax.broadcasted_iota(jnp.int32, (ZB, W), 1)
        == lax.broadcasted_iota(jnp.int32, (ZB, W), 0) + (y * 4 + z) * ZB
    )
    pick = jnp.where(pick, 1.0, 0.0).astype(BF16)
    etr[t] = mm(pick, enc[...], 1, 1).astype(BF16)
    l_go.wait()
    l_dec.wait()
    l_w = []
    for i in range(NT):
        cols = pl.ds(pl.multiple_of(i * W + c * H, 128), H)
        l_w.append(local(w_h.at[:, cols], wv.at[i]))
    l_att = local(att_h, att)
    gcs[...] = mm(go[...], dec[...], 1, 1).astype(BF16)

    pl.semaphore_wait(barrier, len(partners))

    class TensorGather:
        def __init__(self, blk):
            self.blk = blk
            self.cp = {}

        def push(self, tt, k):
            self.cp[k] = send(self.blk(tt), self.blk(tt), {"tensor": t_to(k % 4 if TG else k)})

        def start(self):
            if not TG:
                for k in order:
                    self.push(t, k)
                return
            self.cp[4] = send(self.blk(t), self.blk(t), {"tensor": t_to(4)})
            for k in (2, 1, 3):
                self.push(t, k)

        def mid(self):
            if TG:
                self.cp[4].wait_recv()
                for k in (6, 5, 7):
                    self.push(t_to(4), k)

        def end(self, ks=arrive):
            for k in ks:
                if not (TG and k == 4):
                    self.cp[k].wait_recv()

    et = TensorGather(lambda tt: etr.at[tt])

    def gc_send():
        return {
            k: send(gcs.at[rows(t_to(k), TB), :], gcr.at[k], {"tensor": t_to(k)}) for k in order
        }

    et.start()
    if GCPOS == 0:
        gc_in = gc_send()
    et.mid()
    if GCPOS == 1:
        gc_in = gc_send()

    t_own = d // 4
    rx, rz = (x + 4 - t_own % 4) % 4, (zl + t_own // 4) % 2
    is_own = jnp.logical_and(rx == 0, rz == 0)
    is_two = jnp.logical_and(rx == 0, rz == 1)
    is_three = rx % 2 == 1
    is_last = rx == 2
    passes_on = rx == 1 + 2 * c
    e_recv = counter[0]
    counter[0] += 1
    e_send = [counter[0] + i for i in range(4)]
    counter[0] += 4

    def e_copy(i, dev):
        return pltpu.make_async_remote_copy(
            src_ref=erow, dst_ref=erow, send_sem=ssem.at[e_send[i]], recv_sem=rsem.at[e_recv],
            device_id={"tensor": dev}, device_id_type=MESH,
        )

    class Tree:
        def __init__(self):
            self.z = e_copy(0, (1 - zl) * 4 + x)
            self.p = e_copy(1, zl * 4 + (x + 1) % 4)
            self.m = e_copy(2, zl * 4 + (x + 3) % 4)
            self.f = e_copy(3, zl * 4 + (x + 4 + sgn) % 4)
            self.at = 0

        def step(self):
            self.at += 1
            if self.at == 1:

                @pl.when(is_own)
                def _():
                    cp = pltpu.make_async_copy(enc_h.at[rows(d % 4, ER), :], erow, lsem.at[19])
                    cp.start()
                    cp.wait()
                    self.z.start()
                    self.p.start()
                    self.m.start()

            elif self.at == 2:

                @pl.when(is_two)
                def _():
                    self.z.wait_recv()
                    self.p.start()
                    self.m.start()

            elif self.at == 3:

                @pl.when(is_three)
                def _():
                    self.z.wait_recv()

                @pl.when(passes_on)
                def _():
                    self.f.start()

            elif self.at == 4:

                @pl.when(is_last)
                def _():
                    self.z.wait_recv()

        def drain(self):
            if self.at == 0:
                return
            while self.at < 4:
                self.step()

            @pl.when(is_own)
            def _():
                self.z.wait_send()

            @pl.when(rx == 0)
            def _():
                self.p.wait_send()
                self.m.wait_send()

            @pl.when(passes_on)
            def _():
                self.f.wait_send()

    tree = Tree()

    def step(at):
        for i in (T1, T2, T3, 4):
            if i == at and not NO_TREE:
                tree.step()

    def chunk_sum(own, recv, copies):
        acc = own[rows(t, TB), :].astype(F32)
        for k in arrive:
            copies[k].wait_recv()
            acc = acc + recv[k].astype(F32)
        return acc.astype(BF16)

    gcg = TensorGather(lambda tt: gcf.at[rows(tt, TB), :])
    total = None
    for k in (0, 4, 1, 3, 2, 5, 7, 6):
        if k:
            et.end((k,))
        else:
            for cp in l_w:
                cp.wait()
        if k == 2 and GCPOS == 2:
            gc_in = gc_send()
        term = mm(etr[t_from(k)], wv[t_from(k)], 1, 1)
        total = term if total is None else total + term
    kacc[...] = total
    ksnd[...] = kacc[:, ot_h].astype(BF16)
    k_core = send(ksnd, krcv, other)
    if GCPOS == 3:
        gc_in = gc_send()

    class Gather:
        def __init__(self, buf):
            self.buf = buf
            self.yc = {}
            self.cc = []

        def push(self, r, dev):
            blk = self.buf.at[c, r]
            return send(blk, blk, dev)

        def y_send(self, k):
            for j in (2, 1, 3):
                self.yc[k, j] = self.push(yz_rows(y, z - k), y_dev(j))

        def start(self):
            self.zc = {k: self.push(yz_rows(y, z), z_dev(k)) for k in (2, 1, 3)}
            self.y_send(0)

        def z_step(self, k):
            self.zc[k].wait_recv()
            self.y_send(k)

        def z_rest(self):
            for k in (1, 3, 2):
                self.z_step(k)
            self.own_row()

        def own_row(self):
            self.cc.append(self.push(y_rows(y), other))

        def y_step(self, j):
            for k in (0, 1, 3, 2):
                self.yc[k, j].wait_recv()
            self.cc.append(self.push(y_rows(y - j), other))

        def y_rest(self):
            for j in (1, 3, 2):
                self.y_step(j)

        def finish(self):
            for cp in self.cc:
                cp.wait_recv()

    class Scatter:
        def __init__(self, lhs_t, right, bufs):
            self.lhs_t, self.right = lhs_t, right
            self.own, self.oth, self.rcv, self.ys, self.yr, self.zs, self.zr, self.zown = bufs

        def core_start(self):
            self.cc = {}
            for j in (2, 1, 3, 0):
                r = y_rows(y + j)
                self.oth[r, :] = mm(self.lhs_t[r, :], self.right[:, ot_h], 1, 0).astype(BF16)
                self.cc[j] = send(self.oth.at[r, :], self.rcv.at[r, :], other)

        def core_own(self):
            for j in (2, 1, 3, 0):
                r = y_rows(y + j)
                self.own[r, :] = mm(self.lhs_t[r, :], self.right[:, me_h], 1, 0)

        def y_send(self, k, j):
            r = rows((z + k) % 4, ZB)
            self.yc[k, j] = send(self.ys.at[j - 1, r, :], self.yr.at[j - 1, r, :], y_dev(j))

        def y_start(self):
            self.yc = {}
            for j in (2, 1, 3):
                r = y_rows(y + j)
                self.cc[j].wait_recv()
                self.ys[j - 1] = (self.own[r, :] + self.rcv[r, :].astype(F32)).astype(BF16)
                if SORD and j == 2:
                    for k in (2, 1, 3, 0):
                        self.y_send(k, j)
            for k in (2, 1, 3, 0):
                for j in (1, 3) if SORD else (2, 1, 3):
                    self.y_send(k, j)
            self.cc[0].wait_recv()

        def z_start(self):
            self.zc = {}
            for k in (2, 1, 3, 0):
                self.z_sum(k)

        def z_sum(self, k):
            if 1:
                r = rows((z + k) % 4, ZB)
                yz = yz_rows(y, z + k)
                val = self.own[yz, :] + self.rcv[yz, :].astype(F32)
                for j in (1, 3, 2):
                    self.yc[k, j].wait_recv()
                    val = val + self.yr[j - 1, r, :].astype(F32)
                if k:
                    self.zs[k - 1] = val.astype(BF16)
                    self.zc[k] = send(self.zs.at[k - 1], self.zr.at[k - 1], z_dev(k))
                else:
                    self.zown[...] = val

        def z_end(self):
            val = self.zown[...]
            for k in (1, 3, 2):
                self.zc[k].wait_recv()
                val = val + self.zr[k - 1].astype(F32)
            return val

    k_core.wait_recv()
    kt[c, yz_rows(y, z)] = (kacc[:, me_h] + krcv[...].astype(F32)).astype(BF16)
    kg = Gather(kt)
    kg.start()
    if GCPOS < 2:
        gcf[rows(t, TB), :] = chunk_sum(gcs, gcr, gc_in)
        gcg.start()
        kg.z_step(1)
        kg.z_step(3)
        gcg.mid()
        kg.z_step(2)
        kg.own_row()
    else:
        kg.z_step(1)
        kg.z_step(3)
        kg.z_step(2)
        kg.own_row()
        step(6)
        gcf[rows(t, TB), :] = chunk_sum(gcs, gcr, gc_in)
        gcg.start()
        gcg.mid()
    step(7)

    l_att.wait()
    ms = Scatter(gct, att, (m0, m1, m2, m3, m4, m5, m6, m7))
    if MYP == 0:
        gcg.end()
        gct[...] = gcf[...].T
        ms.core_start()
        ms.core_own()
        ms.y_start()
    kg.y_step(1)
    kg.y_step(3)
    if MYP >= 1:
        gcg.end()
        gct[...] = gcf[...].T
        ms.core_start()
    kg.y_step(2)
    if MYP == 1:
        ms.core_own()
    if MYP == 2:
        ms.core_own()
        ms.y_start()
    kg.finish()
    step(0)

    cws[...] = (mm(att[:, :H], kt[0], 1, 1) + mm(att[:, H:], kt[1], 1, 1)).astype(BF16)
    cw_in = {
        k: send(cws.at[rows(t_to(k), TB), :], cwr.at[k], {"tensor": t_to(k)}) for k in order
    }
    if MYP == 1:
        ms.y_start()
    ga_v[:, :H] = mm(gcf[...], kt[0], 1, 0).astype(BF16)
    ga_v[:, H:] = mm(gcf[...], kt[1], 1, 0).astype(BF16)
    o_ga = local(ga_v, ga_out)
    if MZP == 0:
        ms.z_start()
    cwf[rows(t, TB), :] = chunk_sum(cws, cwr, cw_in)
    cwg = TensorGather(lambda tt: cwf.at[rows(tt, TB), :])
    cwg.start()
    if MZP == 1:
        ms.z_start()
    cwg.mid()
    step(1)
    if MZP == 2:
        ms.z_start()
    m_block = ms.z_end().astype(BF16)
    mt[c, yz_rows(y, z)] = m_block
    mch[c] = m_block
    m_core = send(mch.at[c], mch.at[c], other)
    mg = Gather(mt)
    mg.start()
    cwg.end()
    step(2)
    cwt[...] = cwf[...].T
    ds = Scatter(cwt, go, (d0, d1, d2, d3, d4, d5, d6, d7))
    ds.core_start()
    ds.core_own()
    if MGP == 0:
        mg.z_step(1)
        mg.z_step(3)
    ds.y_start()
    g_in = {}
    m_core.wait_recv()
    for k in order + (0,):
        val = mm(mch[0], wv[t_to(k), :H, :], 1, 0) + mm(mch[1], wv[t_to(k), H:, :], 1, 0)
        if k:
            gs[k] = val.astype(BF16)
            g_in[k] = send(gs.at[k], gr.at[k], {"tensor": t_to(k)})
        else:
            gsum[...] = val
    step(8)
    if MGP == 1:
        mg.z_step(1)
        mg.z_step(3)
    mg.z_step(2)
    mg.own_row()
    dec_v[...] = mm(cwf[...], dec[...], 1, 0).astype(BF16)
    o_dec = local(dec_v, dec_out)
    step(3)
    ds.zc = {}
    ds.z_sum(2)
    for k in arrive:
        g_in[k].wait_recv()
        gsum[...] += gr[k].astype(F32)
    g_core = send(gsum.at[rows(1 - c, CB), :], gswp, other)
    ds.z_sum(1)
    ds.z_sum(3)
    ds.z_sum(0)
    mg.y_step(1)
    mg.y_step(3)
    mg.y_step(2)
    step(4)
    g_core.wait_recv()
    ge_v[:, me_h] = SCALE * gsum[rows(c, CB), :]
    ge_v[:, ot_h] = SCALE * gswp[...]
    o_ge = local(ge_v, ge_out)
    dsum[...] = ds.z_end()
    d_core = send(dsum.at[rows(1 - c, CB), :], dswp, other)
    mg.finish()
    gw_v[:, :H] = SCALE * mm(erow[...], mt[0], 1, 0)
    gw_v[:, H:] = SCALE * mm(erow[...], mt[1], 1, 0)
    o_gw = local(gw_v, gw_out)
    gd_v[:, me_h] = SCALE * dsum[rows(c, CB), :]
    d_core.wait_recv()
    gd_v[:, ot_h] = SCALE * dswp[...]
    o_gd = local(gd_v, gd_out)

    for cp in sent:
        cp.wait_send()
    tree.drain()
    for cp in (o_ga, o_dec, o_gw, o_ge, o_gd):
        cp.wait()
    assert counter[0] <= N_COPIES, counter


def hand_on(*refs):
    ins, outs, held, sem_in, sem_out = refs[:5], refs[5:10], refs[10:15], refs[15], refs[16]
    pieces = [(2, slice(i * 64, i * 64 + 64)) for i in range(3)]
    pieces += [(a, slice(i * 128, i * 128 + 128)) for a in (0, 1) for i in range(2)]
    pieces += [(a, slice(0, CB)) for a in (3, 4)]
    first = [pltpu.make_async_copy(ins[a].at[r], held[a].at[r], sem_in.at[i]) for i, (a, r) in enumerate(pieces)]
    second = [pltpu.make_async_copy(held[a].at[r], outs[a].at[r], sem_out.at[i]) for i, (a, r) in enumerate(pieces)]
    for cp in first:
        cp.start()
    for one, two in zip(first, second):
        one.wait()
        two.start()
    for cp in second:
        cp.wait()


def scatter_scratch():
    v = pltpu.VMEM
    return [
        v((W, H), F32), v((W, H), BF16), v((W, H), BF16), v((3, YB, H), BF16), v((3, YB, H), BF16),
        v((3, ZB, H), BF16), v((3, ZB, H), BF16), v((ZB, H), F32),
    ]


def body(attended, out_weight, encoder, decoder, grad_out):
    v = pltpu.VMEM
    scratch = (
        [v((TOK, W), BF16), v((NT, W, H), BF16), v((H, W), BF16), v((W, W), BF16), v((TOK, W), BF16)]
        + [v((TOK, W), BF16), v((NT, TB, W), BF16), v((TOK, W), BF16), v((W, TOK), BF16)]
        + [v((NT, ZB, H), BF16), v((ZB, W), F32), v((ZB, H), BF16), v((ZB, H), BF16), v((2, W, H), BF16)]
        + scatter_scratch()
        + [v((2, ZB, H), BF16), v((2, W, H), BF16)]
        + [v((NT, ZB, H), BF16), v((NT, ZB, H), BF16), v((ZB, H), F32), v((CB, H), F32), v((CB, W), F32)]
        + [v((TOK, W), BF16), v((NT, TB, W), BF16), v((TOK, W), BF16), v((W, TOK), BF16)]
        + scatter_scratch()
        + [v((ZB, H), F32), v((CB, H), F32), v((CB, W), F32)]
        + [v((ER, W), BF16), v((TOK, W), BF16), v((TOK, W), BF16), v((ER, W), F32)]
        + [
            pltpu.SemaphoreType.DMA((20,)),
            pltpu.SemaphoreType.DMA((N_COPIES,)),
            pltpu.SemaphoreType.DMA((N_COPIES,)),
        ]
    )
    hbm = pl.BlockSpec(memory_space=pl.ANY)
    shapes = (
        jax.ShapeDtypeStruct((TOK, W), BF16),
        jax.ShapeDtypeStruct((TOK, W), BF16),
        jax.ShapeDtypeStruct((ER, W), F32),
        jax.ShapeDtypeStruct((CB, W), F32),
        jax.ShapeDtypeStruct((CB, W), F32),
    )
    results = pl.pallas_call(
        kernel,
        out_shape=shapes,
        in_specs=[hbm] * 5,
        out_specs=[hbm] * 5,
        scratch_shapes=scratch,
        compiler_params=pltpu.CompilerParams(
            collective_id=0, has_side_effects=True, vmem_limit_bytes=VMEM_LIMIT
        ),
    )(attended, out_weight, encoder, decoder, grad_out)
    decoded, grad_attended, weight_t, encoder_t, grad_decoder = pl.pallas_call(
        hand_on,
        out_shape=shapes,
        in_specs=[hbm] * 5,
        out_specs=[hbm] * 5,
        scratch_shapes=[v(a.shape, a.dtype) for a in shapes]
        + [pltpu.SemaphoreType.DMA((9,))] * 2,
        compiler_params=pltpu.CompilerParams(vmem_limit_bytes=VMEM_LIMIT),
    )(*results)
    return decoded, grad_attended, weight_t.T, encoder_t.T, grad_decoder


def solution(mesh):
    return jax.shard_map(
        body,
        mesh=mesh,
        in_specs=(
            P("dp", "tensor"),
            P("tensor", None),
            P("tensor", None),
            P(None, "tensor"),
            P("dp", "tensor"),
        ),
        out_specs=(
            P("dp", "tensor"),
            P("dp", "tensor"),
            P("tensor", "dp"),
            P("tensor", "dp"),
            P("dp", "tensor"),
        ),
        check_vma=False,
    )
```

```python
import jax
import jax.numpy as jnp
from jax import lax
from jax.experimental import pallas as pl
from jax.experimental.pallas import tpu as pltpu
from jax.sharding import PartitionSpec as P

MESH = pl.DeviceIdType.MESH
F32 = jnp.float32
BF16 = jnp.bfloat16
TOK = 256
W = 768
H = W // 2
NY, NZ, NT = 4, 4, 8
YB = W // NY
ZB = YB // NZ
CB = ZB // 2
TB = TOK // NT
ER = W // 4
SCALE = 1.0 / float(8192) ** 0.5
N_COPIES = 140
VMEM_LIMIT = 62 * 1024 * 1024
T1 = 7
T2 = 2
T3 = 3
NO_TREE = False
TG = True
SORD = True
GCPOS = 2
GO = 1
ZE = 1
MC = 0


def mm(a, b, ca, cb):
    return lax.dot_general(a, b, (((ca,), (cb,)), ((), ())), preferred_element_type=F32)


def kernel(
    att_h, w_h, enc_h, dec_h, go_h,
    dec_out, ga_out, gw_out, ge_out, gd_out,
    att, wv, enc, dec, go,
    gcs, gcr, gcf, gct,
    etr, kacc, ksnd, krcv, kt,
    m0, m1, m2, m3, m4, m5, m6, m7, mch, mt,
    gs, gr, gsum, gswp, ge_v,
    cws, cwr, cwf, cwt,
    d0, d1, d2, d3, d4, d5, d6, d7, dsum, dswp, gd_v,
    erow, dec_v, ga_v, gw_v,
    lsem, ssem, rsem,
):
    d = lax.axis_index("dp")
    t = lax.axis_index("tensor")
    y, z, c = d // 8, (d // 2) % 4, d % 2
    zl, x = t // 4, t % 4
    sgn = 1 - 2 * c

    def dp_dev(yy, zz, cc):
        return {"dp": (yy % 4 * 4 + zz % 4) * 2 + cc}

    other = dp_dev(y, z, 1 - c)

    def y_dev(j):
        return dp_dev(y + j + 4, z, c)

    def z_dev(k):
        return dp_dev(y, z + k, c)

    def t_to(k):
        kz, kx = k // 4, k % 4
        return (1 - zl if kz else zl) * 4 + (x + kx) % 4

    def t_from(k):
        kz, kx = k // 4, k % 4
        return (1 - zl if kz else zl) * 4 + (x + 4 - kx) % 4

    order = (2, 6, 5, 7, 1, 3, 4)
    arrive = (1, 3, 4, 5, 7, 2, 6)

    def half(cc):
        return pl.ds(pl.multiple_of(cc * H, 128), H)

    def rows(i, n):
        return pl.ds(pl.multiple_of(i * n, n), n)

    me_h, ot_h = half(c), half(1 - c)

    def y_rows(yy):
        return rows((yy + 8) % 4, YB)

    def yz_rows(yy, zz):
        return rows((yy + 8) % 4 * 4 + (zz + 8) % 4, ZB)

    counter = [0]
    sent = []

    def remote(src, dst, dev):
        i = counter[0]
        counter[0] += 1
        cp = pltpu.make_async_remote_copy(
            src_ref=src, dst_ref=dst, send_sem=ssem.at[i], recv_sem=rsem.at[i],
            device_id=dev, device_id_type=MESH,
        )
        return cp

    def send(src, dst, dev):
        cp = remote(src, dst, dev)
        cp.start()
        sent.append(cp)
        return cp

    lcount = [0]

    def local(src, dst):
        i = lcount[0]
        lcount[0] += 1
        cp = pltpu.make_async_copy(src, dst, lsem.at[i])
        cp.start()
        return cp

    barrier = pltpu.get_barrier_semaphore()
    partners = (
        [{"tensor": t_to(k)} for k in order]
        + [y_dev(j) for j in (2, 1, 3)]
        + [z_dev(k) for k in (2, 1, 3)]
        + [other]
    )
    for dev in partners:
        pl.semaphore_signal(barrier, inc=1, device_id=dev, device_id_type=MESH)
    l_enc = local(enc_h.at[rows(c, H), :], enc)
    l_go = local(go_h, go)
    l_dec = local(dec_h, dec)

    l_enc.wait()
    pick = (
        lax.broadcasted_iota(jnp.int32, (ZB, W), 1)
        == lax.broadcasted_iota(jnp.int32, (ZB, W), 0) + (y * 4 + z) * ZB
    )
    pick = jnp.where(pick, 1.0, 0.0).astype(BF16)
    etr[t] = mm(pick, enc[...], 1, 1).astype(BF16)
    l_go.wait()
    l_dec.wait()
    l_w = []
    for i in range(NT):
        cols = pl.ds(pl.multiple_of(i * W + c * H, 128), H)
        l_w.append(local(w_h.at[:, cols], wv.at[i]))
    l_att = local(att_h, att)
    gcs[...] = mm(go[...], dec[...], 1, 1).astype(BF16)

    pl.semaphore_wait(barrier, len(partners))

    class TensorGather:
        def __init__(self, blk):
            self.blk = blk
            self.cp = {}

        def push(self, tt, k):
            self.cp[k] = send(self.blk(tt), self.blk(tt), {"tensor": t_to(k % 4 if TG else k)})

        def start(self):
            if not TG:
                for k in order:
                    self.push(t, k)
                return
            self.cp[4] = send(self.blk(t), self.blk(t), {"tensor": t_to(4)})
            for k in (2, 1, 3):
                self.push(t, k)

        def mid(self):
            if TG:
                self.cp[4].wait_recv()
                for k in (6, 5, 7):
                    self.push(t_to(4), k)

        def end(self, ks=arrive):
            for k in ks:
                if not (TG and k == 4):
                    self.cp[k].wait_recv()

    et = TensorGather(lambda tt: etr.at[tt])

    def gc_send():
        return {
            k: send(gcs.at[rows(t_to(k), TB), :], gcr.at[k], {"tensor": t_to(k)}) for k in order
        }

    et.start()
    if GCPOS == 0:
        gc_in = gc_send()
    et.mid()
    if GCPOS == 1:
        gc_in = gc_send()

    t_own = d // 4
    rx, rz = (x + 4 - t_own % 4) % 4, (zl + t_own // 4) % 2
    is_own = jnp.logical_and(rx == 0, rz == 0)
    is_two = jnp.logical_and(rx == 0, rz == 1)
    is_three = rx % 2 == 1
    is_last = rx == 2
    passes_on = rx == 1 + 2 * c
    e_recv = counter[0]
    counter[0] += 1
    e_send = [counter[0] + i for i in range(4)]
    counter[0] += 4

    def e_copy(i, dev):
        return pltpu.make_async_remote_copy(
            src_ref=erow, dst_ref=erow, send_sem=ssem.at[e_send[i]], recv_sem=rsem.at[e_recv],
            device_id={"tensor": dev}, device_id_type=MESH,
        )

    class Tree:
        def __init__(self):
            self.z = e_copy(0, (1 - zl) * 4 + x)
            self.p = e_copy(1, zl * 4 + (x + 1) % 4)
            self.m = e_copy(2, zl * 4 + (x + 3) % 4)
            self.f = e_copy(3, zl * 4 + (x + 4 + sgn) % 4)
            self.at = 0

        def step(self):
            self.at += 1
            if self.at == 1:

                @pl.when(is_own)
                def _():
                    cp = pltpu.make_async_copy(enc_h.at[rows(d % 4, ER), :], erow, lsem.at[19])
                    cp.start()
                    cp.wait()
                    self.z.start()
                    self.p.start()
                    self.m.start()

            elif self.at == 2:

                @pl.when(is_two)
                def _():
                    self.z.wait_recv()
                    self.p.start()
                    self.m.start()

            elif self.at == 3:

                @pl.when(is_three)
                def _():
                    self.z.wait_recv()

                @pl.when(passes_on)
                def _():
                    self.f.start()

            elif self.at == 4:

                @pl.when(is_last)
                def _():
                    self.z.wait_recv()

        def drain(self):
            if self.at == 0:
                return
            while self.at < 4:
                self.step()

            @pl.when(is_own)
            def _():
                self.z.wait_send()

            @pl.when(rx == 0)
            def _():
                self.p.wait_send()
                self.m.wait_send()

            @pl.when(passes_on)
            def _():
                self.f.wait_send()

    tree = Tree()

    def step(at):
        for i in (T1, T2, T3, 4):
            if i == at and not NO_TREE:
                tree.step()

    def chunk_sum(own, recv, copies):
        acc = own[rows(t, TB), :].astype(F32)
        for k in arrive:
            copies[k].wait_recv()
            acc = acc + recv[k].astype(F32)
        return acc.astype(BF16)

    gcg = TensorGather(lambda tt: gcf.at[rows(tt, TB), :])
    total = None
    for k in (0, 4, 1, 3, 2, 5, 7, 6):
        if k:
            et.end((k,))
        else:
            for cp in l_w:
                cp.wait()
        if k == 2 and GCPOS == 2:
            gc_in = gc_send()
        term = mm(etr[t_from(k)], wv[t_from(k)], 1, 1)
        total = term if total is None else total + term
    kacc[...] = total
    ksnd[...] = kacc[:, ot_h].astype(BF16)
    k_core = send(ksnd, krcv, other)
    if GCPOS == 3:
        gc_in = gc_send()

    class Gather:
        def __init__(self, buf):
            self.buf = buf
            self.yc = {}
            self.cc = []

        def push(self, r, dev):
            blk = self.buf.at[c, r]
            return send(blk, blk, dev)

        def y_send(self, k):
            for j in (2, 1, 3):
                self.yc[k, j] = self.push(yz_rows(y, z - k), y_dev(j))

        def start(self):
            self.zc = {k: self.push(yz_rows(y, z), z_dev(k)) for k in (2, 1, 3)}
            self.y_send(0)

        def z_step(self, k):
            self.zc[k].wait_recv()
            self.y_send(k)

        def z_rest(self):
            for k in (1, 3, 2):
                self.z_step(k)
            self.own_row()

        def own_row(self):
            self.cc.append(self.push(y_rows(y), other))

        def y_step(self, j):
            for k in (0, 1, 3, 2):
                self.yc[k, j].wait_recv()
            self.cc.append(self.push(y_rows(y - j), other))

        def y_rest(self):
            for j in (1, 3, 2):
                self.y_step(j)

        def finish(self):
            for cp in self.cc:
                cp.wait_recv()

    class Scatter:
        def __init__(self, lhs_t, right, bufs):
            self.lhs_t, self.right = lhs_t, right
            self.own, self.oth, self.rcv, self.ys, self.yr, self.zs, self.zr, self.zown = bufs

        def core_start(self):
            self.cc = {}
            for j in (2, 1, 3, 0):
                r = y_rows(y + j)
                self.oth[r, :] = mm(self.lhs_t[r, :], self.right[:, ot_h], 1, 0).astype(BF16)
                self.cc[j] = send(self.oth.at[r, :], self.rcv.at[r, :], other)

        def core_own(self):
            for j in (2, 1, 3, 0):
                r = y_rows(y + j)
                self.own[r, :] = mm(self.lhs_t[r, :], self.right[:, me_h], 1, 0)

        def y_send(self, k, j):
            r = rows((z + k) % 4, ZB)
            self.yc[k, j] = send(self.ys.at[j - 1, r, :], self.yr.at[j - 1, r, :], y_dev(j))

        def y_start(self):
            self.yc = {}
            for j in (2, 1, 3):
                r = y_rows(y + j)
                self.cc[j].wait_recv()
                self.ys[j - 1] = (self.own[r, :] + self.rcv[r, :].astype(F32)).astype(BF16)
                if SORD and j == 2:
                    for k in (2, 1, 3, 0):
                        self.y_send(k, j)
            for k in (2, 1, 3, 0):
                for j in (1, 3) if SORD else (2, 1, 3):
                    self.y_send(k, j)
            self.cc[0].wait_recv()

        def z_start(self):
            self.zc = {}
            for k in (2, 1, 3, 0):
                self.z_sum(k)

        def z_sum(self, k):
            if 1:
                r = rows((z + k) % 4, ZB)
                yz = yz_rows(y, z + k)
                val = self.own[yz, :] + self.rcv[yz, :].astype(F32)
                for j in (1, 3, 2):
                    self.yc[k, j].wait_recv()
                    val = val + self.yr[j - 1, r, :].astype(F32)
                if k:
                    self.zs[k - 1] = val.astype(BF16)
                    self.zc[k] = send(self.zs.at[k - 1], self.zr.at[k - 1], z_dev(k))
                else:
                    self.zown[...] = val

        def z_end(self):
            val = self.zown[...]
            for k in (1, 3, 2):
                self.zc[k].wait_recv()
                val = val + self.zr[k - 1].astype(F32)
            return val

    k_core.wait_recv()
    kt[c, yz_rows(y, z)] = (kacc[:, me_h] + krcv[...].astype(F32)).astype(BF16)
    kg = Gather(kt)
    kg.start()
    if GO == 1:
        gcf[rows(t, TB), :] = chunk_sum(gcs, gcr, gc_in)
        gcg.start()
        kg.z_step(1)
        kg.z_step(3)
        gcg.mid()
        kg.z_step(2)
        kg.own_row()
    else:
        kg.z_step(1)
        kg.z_step(3)
        kg.z_step(2)
        kg.own_row()
        gcf[rows(t, TB), :] = chunk_sum(gcs, gcr, gc_in)
        gcg.start()
        gcg.mid()
    step(7)

    kg.y_step(1)
    kg.y_step(3)
    kg.y_step(2)
    kg.finish()

    l_att.wait()
    cws[...] = (mm(att[:, :H], kt[0], 1, 1) + mm(att[:, H:], kt[1], 1, 1)).astype(BF16)
    cw_in = {
        k: send(cws.at[rows(t_to(k), TB), :], cwr.at[k], {"tensor": t_to(k)}) for k in order
    }
    gcg.end()
    step(9)
    gct[...] = gcf[...].T
    ms = Scatter(gct, att, (m0, m1, m2, m3, m4, m5, m6, m7))
    ms.core_start()
    ms.core_own()
    ms.y_start()
    ga_v[:, :H] = mm(gcf[...], kt[0], 1, 0).astype(BF16)
    ga_v[:, H:] = mm(gcf[...], kt[1], 1, 0).astype(BF16)
    o_ga = local(ga_v, ga_out)
    cwf[rows(t, TB), :] = chunk_sum(cws, cwr, cw_in)
    cwg = TensorGather(lambda tt: cwf.at[rows(tt, TB), :])
    cwg.start()
    if MC == 0:
        cwg.mid()
    ms.z_start()
    if MC == 1:
        cwg.mid()
    step(1)
    mg = Gather(mt)

    def m_done():
        m_block = ms.z_end().astype(BF16)
        mt[c, yz_rows(y, z)] = m_block
        mch[c] = m_block
        mg.m_core = send(mch.at[c], mch.at[c], other)
        mg.start()

    if ZE == 0:
        m_done()
    cwg.end()
    step(2)
    cwt[...] = cwf[...].T
    ds = Scatter(cwt, go, (d0, d1, d2, d3, d4, d5, d6, d7))
    ds.core_start()
    if ZE == 1:
        m_done()
    ds.core_own()
    ds.y_start()
    if ZE == 2:
        m_done()
    step(10)
    g_in = {}
    mg.m_core.wait_recv()
    for k in order + (0,):
        val = mm(mch[0], wv[t_to(k), :H, :], 1, 0) + mm(mch[1], wv[t_to(k), H:, :], 1, 0)
        if k:
            gs[k] = val.astype(BF16)
            g_in[k] = send(gs.at[k], gr.at[k], {"tensor": t_to(k)})
        else:
            gsum[...] = val
    step(8)
    mg.z_step(1)
    mg.z_step(3)
    mg.z_step(2)
    mg.own_row()
    dec_v[...] = mm(cwf[...], dec[...], 1, 0).astype(BF16)
    o_dec = local(dec_v, dec_out)
    step(3)
    ds.zc = {}
    ds.z_sum(2)
    for k in arrive:
        g_in[k].wait_recv()
        gsum[...] += gr[k].astype(F32)
    g_core = send(gsum.at[rows(1 - c, CB), :], gswp, other)
    ds.z_sum(1)
    ds.z_sum(3)
    ds.z_sum(0)
    mg.y_step(1)
    mg.y_step(3)
    mg.y_step(2)
    step(4)
    g_core.wait_recv()
    ge_v[:, me_h] = SCALE * gsum[rows(c, CB), :]
    ge_v[:, ot_h] = SCALE * gswp[...]
    o_ge = local(ge_v, ge_out)
    dsum[...] = ds.z_end()
    d_core = send(dsum.at[rows(1 - c, CB), :], dswp, other)
    mg.finish()
    gw_v[:, :H] = SCALE * mm(erow[...], mt[0], 1, 0)
    gw_v[:, H:] = SCALE * mm(erow[...], mt[1], 1, 0)
    o_gw = local(gw_v, gw_out)
    gd_v[:, me_h] = SCALE * dsum[rows(c, CB), :]
    d_core.wait_recv()
    gd_v[:, ot_h] = SCALE * dswp[...]
    o_gd = local(gd_v, gd_out)

    for cp in sent:
        cp.wait_send()
    tree.drain()
    for cp in (o_ga, o_dec, o_gw, o_ge, o_gd):
        cp.wait()
    assert counter[0] <= N_COPIES, counter


def hand_on(*refs):
    ins, outs, held, sem_in, sem_out = refs[:5], refs[5:10], refs[10:15], refs[15], refs[16]
    pieces = [(2, slice(i * 64, i * 64 + 64)) for i in range(3)]
    pieces += [(a, slice(i * 128, i * 128 + 128)) for a in (0, 1) for i in range(2)]
    pieces += [(a, slice(0, CB)) for a in (3, 4)]
    first = [pltpu.make_async_copy(ins[a].at[r], held[a].at[r], sem_in.at[i]) for i, (a, r) in enumerate(pieces)]
    second = [pltpu.make_async_copy(held[a].at[r], outs[a].at[r], sem_out.at[i]) for i, (a, r) in enumerate(pieces)]
    for cp in first:
        cp.start()
    for one, two in zip(first, second):
        one.wait()
        two.start()
    for cp in second:
        cp.wait()


def scatter_scratch():
    v = pltpu.VMEM
    return [
        v((W, H), F32), v((W, H), BF16), v((W, H), BF16), v((3, YB, H), BF16), v((3, YB, H), BF16),
        v((3, ZB, H), BF16), v((3, ZB, H), BF16), v((ZB, H), F32),
    ]


def body(attended, out_weight, encoder, decoder, grad_out):
    v = pltpu.VMEM
    scratch = (
        [v((TOK, W), BF16), v((NT, W, H), BF16), v((H, W), BF16), v((W, W), BF16), v((TOK, W), BF16)]
        + [v((TOK, W), BF16), v((NT, TB, W), BF16), v((TOK, W), BF16), v((W, TOK), BF16)]
        + [v((NT, ZB, H), BF16), v((ZB, W), F32), v((ZB, H), BF16), v((ZB, H), BF16), v((2, W, H), BF16)]
        + scatter_scratch()
        + [v((2, ZB, H), BF16), v((2, W, H), BF16)]
        + [v((NT, ZB, H), BF16), v((NT, ZB, H), BF16), v((ZB, H), F32), v((CB, H), F32), v((CB, W), F32)]
        + [v((TOK, W), BF16), v((NT, TB, W), BF16), v((TOK, W), BF16), v((W, TOK), BF16)]
        + scatter_scratch()
        + [v((ZB, H), F32), v((CB, H), F32), v((CB, W), F32)]
        + [v((ER, W), BF16), v((TOK, W), BF16), v((TOK, W), BF16), v((ER, W), F32)]
        + [
            pltpu.SemaphoreType.DMA((20,)),
            pltpu.SemaphoreType.DMA((N_COPIES,)),
            pltpu.SemaphoreType.DMA((N_COPIES,)),
        ]
    )
    hbm = pl.BlockSpec(memory_space=pl.ANY)
    shapes = (
        jax.ShapeDtypeStruct((TOK, W), BF16),
        jax.ShapeDtypeStruct((TOK, W), BF16),
        jax.ShapeDtypeStruct((ER, W), F32),
        jax.ShapeDtypeStruct((CB, W), F32),
        jax.ShapeDtypeStruct((CB, W), F32),
    )
    results = pl.pallas_call(
        kernel,
        out_shape=shapes,
        in_specs=[hbm] * 5,
        out_specs=[hbm] * 5,
        scratch_shapes=scratch,
        compiler_params=pltpu.CompilerParams(
            collective_id=0, has_side_effects=True, vmem_limit_bytes=VMEM_LIMIT
        ),
    )(attended, out_weight, encoder, decoder, grad_out)
    decoded, grad_attended, weight_t, encoder_t, grad_decoder = pl.pallas_call(
        hand_on,
        out_shape=shapes,
        in_specs=[hbm] * 5,
        out_specs=[hbm] * 5,
        scratch_shapes=[v(a.shape, a.dtype) for a in shapes]
        + [pltpu.SemaphoreType.DMA((9,))] * 2,
        compiler_params=pltpu.CompilerParams(vmem_limit_bytes=VMEM_LIMIT),
    )(*results)
    return decoded, grad_attended, weight_t.T, encoder_t.T, grad_decoder


def solution(mesh):
    return jax.shard_map(
        body,
        mesh=mesh,
        in_specs=(
            P("dp", "tensor"),
            P("tensor", None),
            P("tensor", None),
            P(None, "tensor"),
            P("dp", "tensor"),
        ),
        out_specs=(
            P("dp", "tensor"),
            P("dp", "tensor"),
            P("tensor", "dp"),
            P("tensor", "dp"),
            P("dp", "tensor"),
        ),
        check_vma=False,
    )
```

```python
import jax
import jax.numpy as jnp
from jax import lax
from jax.experimental import pallas as pl
from jax.experimental.pallas import tpu as pltpu
from jax.sharding import PartitionSpec as P

MESH = pl.DeviceIdType.MESH
F32 = jnp.float32
BF16 = jnp.bfloat16
TOK = 256
W = 768
H = W // 2
NY, NZ, NT = 4, 4, 8
YB = W // NY
ZB = YB // NZ
CB = ZB // 2
TB = TOK // NT
ER = W // 4
SCALE = 1.0 / float(8192) ** 0.5
N_COPIES = 140
VMEM_LIMIT = 60 * 1024 * 1024
T1 = 7
T2 = 2
T3 = 3
NO_TREE = False
TG = True
SORD = True
GCPOS = 2
GO = 1
ZE = 1
MC = 0


def mm(a, b, ca, cb):
    return lax.dot_general(a, b, (((ca,), (cb,)), ((), ())), preferred_element_type=F32)


def kernel(
    att_h, w_h, enc_h, dec_h, go_h,
    dec_out, ga_out, gw_out, ge_out, gd_out,
    att, wv, enc, dec, go,
    gcs, gcr, gcf, gct,
    etr, kacc, ksnd, krcv, kt,
    m0, m1, m2, m3, m4, m5, m6, m7, mch, mt,
    gs, gr, gsum, gswp,
    cws, cwr, cwf, cwt,
    d0, d1, d2, d3, d4, d5, d6, d7, dsum, dswp,
    erow,
    lsem, ssem, rsem,
):
    d = lax.axis_index("dp")
    t = lax.axis_index("tensor")
    y, z, c = d // 8, (d // 2) % 4, d % 2
    zl, x = t // 4, t % 4
    sgn = 1 - 2 * c

    def dp_dev(yy, zz, cc):
        return {"dp": (yy % 4 * 4 + zz % 4) * 2 + cc}

    other = dp_dev(y, z, 1 - c)

    def y_dev(j):
        return dp_dev(y + j + 4, z, c)

    def z_dev(k):
        return dp_dev(y, z + k, c)

    def t_to(k):
        kz, kx = k // 4, k % 4
        return (1 - zl if kz else zl) * 4 + (x + kx) % 4

    def t_from(k):
        kz, kx = k // 4, k % 4
        return (1 - zl if kz else zl) * 4 + (x + 4 - kx) % 4

    order = (2, 6, 5, 7, 1, 3, 4)
    arrive = (1, 3, 4, 5, 7, 2, 6)

    def half(cc):
        return pl.ds(pl.multiple_of(cc * H, 128), H)

    def rows(i, n):
        return pl.ds(pl.multiple_of(i * n, n), n)

    me_h, ot_h = half(c), half(1 - c)

    def y_rows(yy):
        return rows((yy + 8) % 4, YB)

    def yz_rows(yy, zz):
        return rows((yy + 8) % 4 * 4 + (zz + 8) % 4, ZB)

    counter = [0]
    sent = []

    def remote(src, dst, dev):
        i = counter[0]
        counter[0] += 1
        cp = pltpu.make_async_remote_copy(
            src_ref=src, dst_ref=dst, send_sem=ssem.at[i], recv_sem=rsem.at[i],
            device_id=dev, device_id_type=MESH,
        )
        return cp

    def send(src, dst, dev):
        cp = remote(src, dst, dev)
        cp.start()
        sent.append(cp)
        return cp

    lcount = [0]

    def local(src, dst):
        i = lcount[0]
        lcount[0] += 1
        cp = pltpu.make_async_copy(src, dst, lsem.at[i])
        cp.start()
        return cp

    barrier = pltpu.get_barrier_semaphore()
    partners = (
        [{"tensor": t_to(k)} for k in order]
        + [y_dev(j) for j in (2, 1, 3)]
        + [z_dev(k) for k in (2, 1, 3)]
        + [other]
    )
    for dev in partners:
        pl.semaphore_signal(barrier, inc=1, device_id=dev, device_id_type=MESH)
    l_enc = local(enc_h.at[rows(c, H), :], enc)
    l_go = local(go_h, go)
    l_dec = local(dec_h, dec)

    l_enc.wait()
    pick = (
        lax.broadcasted_iota(jnp.int32, (ZB, W), 1)
        == lax.broadcasted_iota(jnp.int32, (ZB, W), 0) + (y * 4 + z) * ZB
    )
    pick = jnp.where(pick, 1.0, 0.0).astype(BF16)
    etr[t] = mm(pick, enc[...], 1, 1).astype(BF16)
    l_go.wait()
    l_dec.wait()
    l_w = []
    for i in range(NT):
        cols = pl.ds(pl.multiple_of(i * W + c * H, 128), H)
        l_w.append(local(w_h.at[:, cols], wv.at[i]))
    l_att = local(att_h, att)
    gcs[...] = mm(go[...], dec[...], 1, 1).astype(BF16)

    pl.semaphore_wait(barrier, len(partners))

    class TensorGather:
        def __init__(self, blk):
            self.blk = blk
            self.cp = {}

        def push(self, tt, k):
            self.cp[k] = send(self.blk(tt), self.blk(tt), {"tensor": t_to(k % 4 if TG else k)})

        def start(self):
            if not TG:
                for k in order:
                    self.push(t, k)
                return
            self.cp[4] = send(self.blk(t), self.blk(t), {"tensor": t_to(4)})
            for k in (2, 1, 3):
                self.push(t, k)

        def mid(self):
            if TG:
                self.cp[4].wait_recv()
                for k in (6, 5, 7):
                    self.push(t_to(4), k)

        def end(self, ks=arrive):
            for k in ks:
                if not (TG and k == 4):
                    self.cp[k].wait_recv()

    et = TensorGather(lambda tt: etr.at[tt])

    def gc_send():
        return {
            k: send(gcs.at[rows(t_to(k), TB), :], gcr.at[k], {"tensor": t_to(k)}) for k in order
        }

    et.start()
    if GCPOS == 0:
        gc_in = gc_send()
    et.mid()
    if GCPOS == 1:
        gc_in = gc_send()

    t_own = d // 4
    rx, rz = (x + 4 - t_own % 4) % 4, (zl + t_own // 4) % 2
    is_own = jnp.logical_and(rx == 0, rz == 0)
    is_two = jnp.logical_and(rx == 0, rz == 1)
    is_three = rx % 2 == 1
    is_last = rx == 2
    passes_on = rx == 1 + 2 * c
    e_recv = counter[0]
    counter[0] += 1
    e_send = [counter[0] + i for i in range(4)]
    counter[0] += 4

    def e_copy(i, dev):
        return pltpu.make_async_remote_copy(
            src_ref=erow, dst_ref=erow, send_sem=ssem.at[e_send[i]], recv_sem=rsem.at[e_recv],
            device_id={"tensor": dev}, device_id_type=MESH,
        )

    class Tree:
        def __init__(self):
            self.z = e_copy(0, (1 - zl) * 4 + x)
            self.p = e_copy(1, zl * 4 + (x + 1) % 4)
            self.m = e_copy(2, zl * 4 + (x + 3) % 4)
            self.f = e_copy(3, zl * 4 + (x + 4 + sgn) % 4)
            self.at = 0

        def step(self):
            self.at += 1
            if self.at == 1:

                @pl.when(is_own)
                def _():
                    cp = pltpu.make_async_copy(enc_h.at[rows(d % 4, ER), :], erow, lsem.at[19])
                    cp.start()
                    cp.wait()
                    self.z.start()
                    self.p.start()
                    self.m.start()

            elif self.at == 2:

                @pl.when(is_two)
                def _():
                    self.z.wait_recv()
                    self.p.start()
                    self.m.start()

            elif self.at == 3:

                @pl.when(is_three)
                def _():
                    self.z.wait_recv()

                @pl.when(passes_on)
                def _():
                    self.f.start()

            elif self.at == 4:

                @pl.when(is_last)
                def _():
                    self.z.wait_recv()

        def drain(self):
            if self.at == 0:
                return
            while self.at < 4:
                self.step()

            @pl.when(is_own)
            def _():
                self.z.wait_send()

            @pl.when(rx == 0)
            def _():
                self.p.wait_send()
                self.m.wait_send()

            @pl.when(passes_on)
            def _():
                self.f.wait_send()

    tree = Tree()

    def step(at):
        for i in (T1, T2, T3, 4):
            if i == at and not NO_TREE:
                tree.step()

    def chunk_sum(own, recv, copies):
        acc = own[rows(t, TB), :].astype(F32)
        for k in arrive:
            copies[k].wait_recv()
            acc = acc + recv[k].astype(F32)
        return acc.astype(BF16)

    gcg = TensorGather(lambda tt: gcf.at[rows(tt, TB), :])
    total = None
    for k in (0, 4, 1, 3, 2, 5, 7, 6):
        if k:
            et.end((k,))
        else:
            for cp in l_w:
                cp.wait()
        if k == 2 and GCPOS == 2:
            gc_in = gc_send()
        term = mm(etr[t_from(k)], wv[t_from(k)], 1, 1)
        total = term if total is None else total + term
    kacc[...] = total
    ksnd[...] = kacc[:, ot_h].astype(BF16)
    k_core = send(ksnd, krcv, other)
    if GCPOS == 3:
        gc_in = gc_send()

    class Gather:
        def __init__(self, buf):
            self.buf = buf
            self.yc = {}
            self.cc = []

        def push(self, r, dev):
            blk = self.buf.at[c, r]
            return send(blk, blk, dev)

        def y_send(self, k):
            for j in (2, 1, 3):
                self.yc[k, j] = self.push(yz_rows(y, z - k), y_dev(j))

        def start(self):
            self.zc = {k: self.push(yz_rows(y, z), z_dev(k)) for k in (2, 1, 3)}
            self.y_send(0)

        def z_step(self, k):
            self.zc[k].wait_recv()
            self.y_send(k)

        def z_rest(self):
            for k in (1, 3, 2):
                self.z_step(k)
            self.own_row()

        def own_row(self):
            self.cc.append(self.push(y_rows(y), other))

        def y_step(self, j):
            for k in (0, 1, 3, 2):
                self.yc[k, j].wait_recv()
            self.cc.append(self.push(y_rows(y - j), other))

        def y_rest(self):
            for j in (1, 3, 2):
                self.y_step(j)

        def finish(self):
            for cp in self.cc:
                cp.wait_recv()

    class Scatter:
        def __init__(self, lhs_t, right, bufs):
            self.lhs_t, self.right = lhs_t, right
            self.own, self.oth, self.rcv, self.ys, self.yr, self.zs, self.zr, self.zown = bufs

        def core_start(self):
            self.cc = {}
            for j in (2, 1, 3, 0):
                r = y_rows(y + j)
                self.oth[r, :] = mm(self.lhs_t[r, :], self.right[:, ot_h], 1, 0).astype(BF16)
                self.cc[j] = send(self.oth.at[r, :], self.rcv.at[r, :], other)

        def core_own(self):
            for j in (2, 1, 3, 0):
                r = y_rows(y + j)
                self.own[r, :] = mm(self.lhs_t[r, :], self.right[:, me_h], 1, 0)

        def y_send(self, k, j):
            r = rows((z + k) % 4, ZB)
            self.yc[k, j] = send(self.ys.at[j - 1, r, :], self.yr.at[j - 1, r, :], y_dev(j))

        def y_start(self):
            self.yc = {}
            for j in (2, 1, 3):
                r = y_rows(y + j)
                self.cc[j].wait_recv()
                self.ys[j - 1] = (self.own[r, :] + self.rcv[r, :].astype(F32)).astype(BF16)
                if SORD and j == 2:
                    for k in (2, 1, 3, 0):
                        self.y_send(k, j)
            for k in (2, 1, 3, 0):
                for j in (1, 3) if SORD else (2, 1, 3):
                    self.y_send(k, j)
            self.cc[0].wait_recv()

        def z_start(self):
            self.zc = {}
            for k in (2, 1, 3, 0):
                self.z_sum(k)

        def z_sum(self, k):
            if 1:
                r = rows((z + k) % 4, ZB)
                yz = yz_rows(y, z + k)
                val = self.own[yz, :] + self.rcv[yz, :].astype(F32)
                for j in (1, 3, 2):
                    self.yc[k, j].wait_recv()
                    val = val + self.yr[j - 1, r, :].astype(F32)
                if k:
                    self.zs[k - 1] = val.astype(BF16)
                    self.zc[k] = send(self.zs.at[k - 1], self.zr.at[k - 1], z_dev(k))
                else:
                    self.zown[...] = val

        def z_end(self):
            val = self.zown[...]
            for k in (1, 3, 2):
                self.zc[k].wait_recv()
                val = val + self.zr[k - 1].astype(F32)
            return val

    k_core.wait_recv()
    kt[c, yz_rows(y, z)] = (kacc[:, me_h] + krcv[...].astype(F32)).astype(BF16)
    kg = Gather(kt)
    kg.start()
    if GO == 1:
        gcf[rows(t, TB), :] = chunk_sum(gcs, gcr, gc_in)
        gcg.start()
        kg.z_step(1)
        kg.z_step(3)
        gcg.mid()
        kg.z_step(2)
        kg.own_row()
    else:
        kg.z_step(1)
        kg.z_step(3)
        kg.z_step(2)
        kg.own_row()
        gcf[rows(t, TB), :] = chunk_sum(gcs, gcr, gc_in)
        gcg.start()
        gcg.mid()
    step(7)

    kg.y_step(1)
    kg.y_step(3)
    kg.y_step(2)
    kg.finish()

    l_att.wait()
    cws[...] = (mm(att[:, :H], kt[0], 1, 1) + mm(att[:, H:], kt[1], 1, 1)).astype(BF16)
    cw_in = {
        k: send(cws.at[rows(t_to(k), TB), :], cwr.at[k], {"tensor": t_to(k)}) for k in order
    }
    gcg.end()
    step(9)
    gct[...] = gcf[...].T
    ms = Scatter(gct, att, (m0, m1, m2, m3, m4, m5, m6, m7))
    ms.core_start()
    ms.core_own()
    ms.y_start()
    ga_out[:, :H] = mm(gcf[...], kt[0], 1, 0).astype(BF16)
    ga_out[:, H:] = mm(gcf[...], kt[1], 1, 0).astype(BF16)
    cwf[rows(t, TB), :] = chunk_sum(cws, cwr, cw_in)
    cwg = TensorGather(lambda tt: cwf.at[rows(tt, TB), :])
    cwg.start()
    if MC == 0:
        cwg.mid()
    ms.z_start()
    if MC == 1:
        cwg.mid()
    step(1)
    mg = Gather(mt)

    def m_done():
        m_block = ms.z_end().astype(BF16)
        mt[c, yz_rows(y, z)] = m_block
        mch[c] = m_block
        mg.m_core = send(mch.at[c], mch.at[c], other)
        mg.start()

    if ZE == 0:
        m_done()
    cwg.end()
    step(2)
    cwt[...] = cwf[...].T
    ds = Scatter(cwt, go, (d0, d1, d2, d3, d4, d5, d6, d7))
    ds.core_start()
    if ZE == 1:
        m_done()
    ds.core_own()
    ds.y_start()
    if ZE == 2:
        m_done()
    step(10)
    g_in = {}
    mg.m_core.wait_recv()
    for k in order + (0,):
        val = mm(mch[0], wv[t_to(k), :H, :], 1, 0) + mm(mch[1], wv[t_to(k), H:, :], 1, 0)
        if k:
            gs[k] = val.astype(BF16)
            g_in[k] = send(gs.at[k], gr.at[k], {"tensor": t_to(k)})
        else:
            gsum[...] = val
    step(8)
    mg.z_step(1)
    mg.z_step(3)
    mg.z_step(2)
    mg.own_row()
    dec_out[...] = mm(cwf[...], dec[...], 1, 0).astype(BF16)
    step(3)
    ds.zc = {}
    ds.z_sum(2)
    for k in arrive:
        g_in[k].wait_recv()
        gsum[...] += gr[k].astype(F32)
    g_core = send(gsum.at[rows(1 - c, CB), :], gswp, other)
    ds.z_sum(1)
    ds.z_sum(3)
    ds.z_sum(0)
    mg.y_step(1)
    mg.y_step(3)
    mg.y_step(2)
    step(4)
    g_core.wait_recv()
    ge_out[:, me_h] = SCALE * gsum[rows(c, CB), :]
    ge_out[:, ot_h] = SCALE * gswp[...]
    dsum[...] = ds.z_end()
    d_core = send(dsum.at[rows(1 - c, CB), :], dswp, other)
    mg.finish()
    gw_out[:, :H] = SCALE * mm(erow[...], mt[0], 1, 0)
    gw_out[:, H:] = SCALE * mm(erow[...], mt[1], 1, 0)
    gd_out[:, me_h] = SCALE * dsum[rows(c, CB), :]
    d_core.wait_recv()
    gd_out[:, ot_h] = SCALE * dswp[...]

    for cp in sent:
        cp.wait_send()
    tree.drain()
    assert counter[0] <= N_COPIES, counter


def hand_on(*refs):
    copies = [pltpu.make_async_copy(refs[i], refs[5 + i], refs[10].at[i]) for i in range(5)]
    for cp in copies:
        cp.start()
    for cp in copies:
        cp.wait()


def scatter_scratch():
    v = pltpu.VMEM
    return [
        v((W, H), F32), v((W, H), BF16), v((W, H), BF16), v((3, YB, H), BF16), v((3, YB, H), BF16),
        v((3, ZB, H), BF16), v((3, ZB, H), BF16), v((ZB, H), F32),
    ]


def body(attended, out_weight, encoder, decoder, grad_out):
    v = pltpu.VMEM
    scratch = (
        [v((TOK, W), BF16), v((NT, W, H), BF16), v((H, W), BF16), v((W, W), BF16), v((TOK, W), BF16)]
        + [v((TOK, W), BF16), v((NT, TB, W), BF16), v((TOK, W), BF16), v((W, TOK), BF16)]
        + [v((NT, ZB, H), BF16), v((ZB, W), F32), v((ZB, H), BF16), v((ZB, H), BF16), v((2, W, H), BF16)]
        + scatter_scratch()
        + [v((2, ZB, H), BF16), v((2, W, H), BF16)]
        + [v((NT, ZB, H), BF16), v((NT, ZB, H), BF16), v((ZB, H), F32), v((CB, H), F32)]
        + [v((TOK, W), BF16), v((NT, TB, W), BF16), v((TOK, W), BF16), v((W, TOK), BF16)]
        + scatter_scratch()
        + [v((ZB, H), F32), v((CB, H), F32)]
        + [v((ER, W), BF16)]
        + [
            pltpu.SemaphoreType.DMA((20,)),
            pltpu.SemaphoreType.DMA((N_COPIES,)),
            pltpu.SemaphoreType.DMA((N_COPIES,)),
        ]
    )
    hbm = pl.BlockSpec(memory_space=pl.ANY)
    shapes = (
        jax.ShapeDtypeStruct((TOK, W), BF16),
        jax.ShapeDtypeStruct((TOK, W), BF16),
        jax.ShapeDtypeStruct((ER, W), F32),
        jax.ShapeDtypeStruct((CB, W), F32),
        jax.ShapeDtypeStruct((CB, W), F32),
    )
    results = pl.pallas_call(
        kernel,
        out_shape=tuple(pltpu.VMEM(a.shape, a.dtype) for a in shapes),
        in_specs=[hbm] * 5,
        out_specs=[pl.BlockSpec(memory_space=pltpu.VMEM)] * 5,
        scratch_shapes=scratch,
        compiler_params=pltpu.CompilerParams(
            collective_id=0, has_side_effects=True, vmem_limit_bytes=VMEM_LIMIT
        ),
    )(attended, out_weight, encoder, decoder, grad_out)
    decoded, grad_attended, weight_t, encoder_t, grad_decoder = pl.pallas_call(
        hand_on,
        out_shape=shapes,
        in_specs=[pl.BlockSpec(memory_space=pltpu.VMEM)] * 5,
        out_specs=[hbm] * 5,
        scratch_shapes=[pltpu.SemaphoreType.DMA((5,))],
        compiler_params=pltpu.CompilerParams(vmem_limit_bytes=32 * 1024 * 1024),
    )(*results)
    return decoded, grad_attended, weight_t.T, encoder_t.T, grad_decoder


def solution(mesh):
    return jax.shard_map(
        body,
        mesh=mesh,
        in_specs=(
            P("dp", "tensor"),
            P("tensor", None),
            P("tensor", None),
            P(None, "tensor"),
            P("dp", "tensor"),
        ),
        out_specs=(
            P("dp", "tensor"),
            P("dp", "tensor"),
            P("tensor", "dp"),
            P("tensor", "dp"),
            P("dp", "tensor"),
        ),
        check_vma=False,
    )
```

```python
import jax
import jax.numpy as jnp
from jax import lax
from jax.experimental import pallas as pl
from jax.experimental.pallas import tpu as pltpu
from jax.sharding import PartitionSpec as P

MESH = pl.DeviceIdType.MESH
F32 = jnp.float32
BF16 = jnp.bfloat16
TOK = 256
W = 768
H = W // 2
NY, NZ, NT = 4, 4, 8
YB = W // NY
ZB = YB // NZ
CB = ZB // 2
TB = TOK // NT
ER = W // 4
SCALE = 1.0 / float(8192) ** 0.5
N_COPIES = 140
VMEM_LIMIT = 60 * 1024 * 1024
T1 = 7
T2 = 2
T3 = 3
NO_TREE = False
TG = True
SORD = True
GCPOS = 2
GO = 1
ZE = 1
MC = 0
FL = True


def mm(a, b, ca, cb):
    return lax.dot_general(a, b, (((ca,), (cb,)), ((), ())), preferred_element_type=F32)


def kernel(
    att_h, w_h, enc_h, dec_h, go_h,
    dec_out, ga_out, gw_out, ge_out, gd_out,
    att, wv, enc, dec, go,
    gcs, gcr, gcf, gct,
    etr, kacc, ksnd, krcv, kt,
    m0, m1, m2, m3, m4, m5, m6, m7, mch, mt,
    gs, gr, gsum, gswp,
    cws, cwr, cwf, cwt,
    d0, d1, d2, d3, d4, d5, d6, d7, dsum, dswp,
    erow,
    lsem, ssem, rsem,
):
    d = lax.axis_index("dp")
    t = lax.axis_index("tensor")
    y, z, c = d // 8, (d // 2) % 4, d % 2
    zl, x = t // 4, t % 4
    sgn = 1 - 2 * c

    def dp_dev(yy, zz, cc):
        return {"dp": (yy % 4 * 4 + zz % 4) * 2 + cc}

    other = dp_dev(y, z, 1 - c)

    def y_dev(j):
        return dp_dev(y + j + 4, z, c)

    def z_dev(k):
        return dp_dev(y, z + k, c)

    def t_to(k):
        kz, kx = k // 4, k % 4
        return (1 - zl if kz else zl) * 4 + (x + kx) % 4

    def t_from(k):
        kz, kx = k // 4, k % 4
        return (1 - zl if kz else zl) * 4 + (x + 4 - kx) % 4

    order = (2, 6, 5, 7, 1, 3, 4)
    arrive = (1, 3, 4, 5, 7, 2, 6)

    def half(cc):
        return pl.ds(pl.multiple_of(cc * H, 128), H)

    def rows(i, n):
        return pl.ds(pl.multiple_of(i * n, n), n)

    me_h, ot_h = half(c), half(1 - c)

    def y_rows(yy):
        return rows((yy + 8) % 4, YB)

    def yz_rows(yy, zz):
        return rows((yy + 8) % 4 * 4 + (zz + 8) % 4, ZB)

    counter = [0]
    sent = []

    def remote(src, dst, dev):
        i = counter[0]
        counter[0] += 1
        cp = pltpu.make_async_remote_copy(
            src_ref=src, dst_ref=dst, send_sem=ssem.at[i], recv_sem=rsem.at[i],
            device_id=dev, device_id_type=MESH,
        )
        return cp

    def send(src, dst, dev):
        cp = remote(src, dst, dev)
        cp.start()
        sent.append(cp)
        return cp

    marks = []

    def mark():
        marks.append(len(sent))

    def flush():
        if FL:
            for cp in sent[: marks[-1]]:
                cp.wait_send()
            del sent[: marks[-1]]

    lcount = [0]

    def local(src, dst):
        i = lcount[0]
        lcount[0] += 1
        cp = pltpu.make_async_copy(src, dst, lsem.at[i])
        cp.start()
        return cp

    barrier = pltpu.get_barrier_semaphore()
    partners = (
        [{"tensor": t_to(k)} for k in order]
        + [y_dev(j) for j in (2, 1, 3)]
        + [z_dev(k) for k in (2, 1, 3)]
        + [other]
    )
    for dev in partners:
        pl.semaphore_signal(barrier, inc=1, device_id=dev, device_id_type=MESH)
    l_enc = local(enc_h.at[rows(c, H), :], enc)
    l_go = local(go_h, go)
    l_dec = local(dec_h, dec)

    l_enc.wait()
    pick = (
        lax.broadcasted_iota(jnp.int32, (ZB, W), 1)
        == lax.broadcasted_iota(jnp.int32, (ZB, W), 0) + (y * 4 + z) * ZB
    )
    pick = jnp.where(pick, 1.0, 0.0).astype(BF16)
    etr[t] = mm(pick, enc[...], 1, 1).astype(BF16)
    l_go.wait()
    l_dec.wait()
    l_w = []
    for i in range(NT):
        cols = pl.ds(pl.multiple_of(i * W + c * H, 128), H)
        l_w.append(local(w_h.at[:, cols], wv.at[i]))
    l_att = local(att_h, att)
    gcs[...] = mm(go[...], dec[...], 1, 1).astype(BF16)

    pl.semaphore_wait(barrier, len(partners))

    class TensorGather:
        def __init__(self, blk):
            self.blk = blk
            self.cp = {}

        def push(self, tt, k):
            self.cp[k] = send(self.blk(tt), self.blk(tt), {"tensor": t_to(k % 4 if TG else k)})

        def start(self):
            if not TG:
                for k in order:
                    self.push(t, k)
                return
            self.cp[4] = send(self.blk(t), self.blk(t), {"tensor": t_to(4)})
            for k in (2, 1, 3):
                self.push(t, k)

        def mid(self):
            if TG:
                self.cp[4].wait_recv()
                for k in (6, 5, 7):
                    self.push(t_to(4), k)

        def end(self, ks=arrive):
            for k in ks:
                if not (TG and k == 4):
                    self.cp[k].wait_recv()

    et = TensorGather(lambda tt: etr.at[tt])

    def gc_send():
        return {
            k: send(gcs.at[rows(t_to(k), TB), :], gcr.at[k], {"tensor": t_to(k)}) for k in order
        }

    et.start()
    if GCPOS == 0:
        gc_in = gc_send()
    et.mid()
    if GCPOS == 1:
        gc_in = gc_send()

    t_own = d // 4
    rx, rz = (x + 4 - t_own % 4) % 4, (zl + t_own // 4) % 2
    is_own = jnp.logical_and(rx == 0, rz == 0)
    is_two = jnp.logical_and(rx == 0, rz == 1)
    is_three = rx % 2 == 1
    is_last = rx == 2
    passes_on = rx == 1 + 2 * c
    e_recv = counter[0]
    counter[0] += 1
    e_send = [counter[0] + i for i in range(4)]
    counter[0] += 4

    def e_copy(i, dev):
        return pltpu.make_async_remote_copy(
            src_ref=erow, dst_ref=erow, send_sem=ssem.at[e_send[i]], recv_sem=rsem.at[e_recv],
            device_id={"tensor": dev}, device_id_type=MESH,
        )

    class Tree:
        def __init__(self):
            self.z = e_copy(0, (1 - zl) * 4 + x)
            self.p = e_copy(1, zl * 4 + (x + 1) % 4)
            self.m = e_copy(2, zl * 4 + (x + 3) % 4)
            self.f = e_copy(3, zl * 4 + (x + 4 + sgn) % 4)
            self.at = 0

        def step(self):
            self.at += 1
            if self.at == 1:

                @pl.when(is_own)
                def _():
                    cp = pltpu.make_async_copy(enc_h.at[rows(d % 4, ER), :], erow, lsem.at[19])
                    cp.start()
                    cp.wait()
                    self.z.start()
                    self.p.start()
                    self.m.start()

            elif self.at == 2:

                @pl.when(is_two)
                def _():
                    self.z.wait_recv()
                    self.p.start()
                    self.m.start()

            elif self.at == 3:

                @pl.when(is_three)
                def _():
                    self.z.wait_recv()

                @pl.when(passes_on)
                def _():
                    self.f.start()

            elif self.at == 4:

                @pl.when(is_last)
                def _():
                    self.z.wait_recv()

        def drain(self):
            if self.at == 0:
                return
            while self.at < 4:
                self.step()

            @pl.when(is_own)
            def _():
                self.z.wait_send()

            @pl.when(rx == 0)
            def _():
                self.p.wait_send()
                self.m.wait_send()

            @pl.when(passes_on)
            def _():
                self.f.wait_send()

    tree = Tree()

    def step(at):
        for i in (T1, T2, T3, 4):
            if i == at and not NO_TREE:
                tree.step()

    def chunk_sum(own, recv, copies):
        acc = own[rows(t, TB), :].astype(F32)
        for k in arrive:
            copies[k].wait_recv()
            acc = acc + recv[k].astype(F32)
        return acc.astype(BF16)

    gcg = TensorGather(lambda tt: gcf.at[rows(tt, TB), :])
    total = None
    for k in (0, 4, 1, 3, 2, 5, 7, 6):
        if k:
            et.end((k,))
        else:
            for cp in l_w:
                cp.wait()
        if k == 2 and GCPOS == 2:
            gc_in = gc_send()
        term = mm(etr[t_from(k)], wv[t_from(k)], 1, 1)
        total = term if total is None else total + term
    kacc[...] = total
    ksnd[...] = kacc[:, ot_h].astype(BF16)
    k_core = send(ksnd, krcv, other)
    if GCPOS == 3:
        gc_in = gc_send()

    class Gather:
        def __init__(self, buf):
            self.buf = buf
            self.yc = {}
            self.cc = []

        def push(self, r, dev):
            blk = self.buf.at[c, r]
            return send(blk, blk, dev)

        def y_send(self, k):
            for j in (2, 1, 3):
                self.yc[k, j] = self.push(yz_rows(y, z - k), y_dev(j))

        def start(self):
            self.zc = {k: self.push(yz_rows(y, z), z_dev(k)) for k in (2, 1, 3)}
            self.y_send(0)

        def z_step(self, k):
            self.zc[k].wait_recv()
            self.y_send(k)

        def z_rest(self):
            for k in (1, 3, 2):
                self.z_step(k)
            self.own_row()

        def own_row(self):
            self.cc.append(self.push(y_rows(y), other))

        def y_step(self, j):
            for k in (0, 1, 3, 2):
                self.yc[k, j].wait_recv()
            self.cc.append(self.push(y_rows(y - j), other))

        def y_rest(self):
            for j in (1, 3, 2):
                self.y_step(j)

        def finish(self):
            for cp in self.cc:
                cp.wait_recv()

    class Scatter:
        def __init__(self, lhs_t, right, bufs):
            self.lhs_t, self.right = lhs_t, right
            self.own, self.oth, self.rcv, self.ys, self.yr, self.zs, self.zr, self.zown = bufs

        def core_start(self):
            self.cc = {}
            for j in (2, 1, 3, 0):
                r = y_rows(y + j)
                self.oth[r, :] = mm(self.lhs_t[r, :], self.right[:, ot_h], 1, 0).astype(BF16)
                self.cc[j] = send(self.oth.at[r, :], self.rcv.at[r, :], other)

        def core_own(self):
            for j in (2, 1, 3, 0):
                r = y_rows(y + j)
                self.own[r, :] = mm(self.lhs_t[r, :], self.right[:, me_h], 1, 0)

        def y_send(self, k, j):
            r = rows((z + k) % 4, ZB)
            self.yc[k, j] = send(self.ys.at[j - 1, r, :], self.yr.at[j - 1, r, :], y_dev(j))

        def y_start(self):
            self.yc = {}
            for j in (2, 1, 3):
                r = y_rows(y + j)
                self.cc[j].wait_recv()
                self.ys[j - 1] = (self.own[r, :] + self.rcv[r, :].astype(F32)).astype(BF16)
                if SORD and j == 2:
                    for k in (2, 1, 3, 0):
                        self.y_send(k, j)
            for k in (2, 1, 3, 0):
                for j in (1, 3) if SORD else (2, 1, 3):
                    self.y_send(k, j)
            self.cc[0].wait_recv()

        def z_start(self):
            self.zc = {}
            for k in (2, 1, 3, 0):
                self.z_sum(k)

        def z_sum(self, k):
            if 1:
                r = rows((z + k) % 4, ZB)
                yz = yz_rows(y, z + k)
                val = self.own[yz, :] + self.rcv[yz, :].astype(F32)
                for j in (1, 3, 2):
                    self.yc[k, j].wait_recv()
                    val = val + self.yr[j - 1, r, :].astype(F32)
                if k:
                    self.zs[k - 1] = val.astype(BF16)
                    self.zc[k] = send(self.zs.at[k - 1], self.zr.at[k - 1], z_dev(k))
                else:
                    self.zown[...] = val

        def z_end(self):
            val = self.zown[...]
            for k in (1, 3, 2):
                self.zc[k].wait_recv()
                val = val + self.zr[k - 1].astype(F32)
            return val

    k_core.wait_recv()
    kt[c, yz_rows(y, z)] = (kacc[:, me_h] + krcv[...].astype(F32)).astype(BF16)
    kg = Gather(kt)
    kg.start()
    if GO == 1:
        gcf[rows(t, TB), :] = chunk_sum(gcs, gcr, gc_in)
        gcg.start()
        kg.z_step(1)
        kg.z_step(3)
        gcg.mid()
        kg.z_step(2)
        kg.own_row()
    else:
        kg.z_step(1)
        kg.z_step(3)
        kg.z_step(2)
        kg.own_row()
        gcf[rows(t, TB), :] = chunk_sum(gcs, gcr, gc_in)
        gcg.start()
        gcg.mid()
    step(7)

    kg.y_step(1)
    kg.y_step(3)
    kg.y_step(2)
    kg.finish()

    l_att.wait()
    cws[...] = (mm(att[:, :H], kt[0], 1, 1) + mm(att[:, H:], kt[1], 1, 1)).astype(BF16)
    cw_in = {
        k: send(cws.at[rows(t_to(k), TB), :], cwr.at[k], {"tensor": t_to(k)}) for k in order
    }
    gcg.end()
    step(9)
    gct[...] = gcf[...].T
    ms = Scatter(gct, att, (m0, m1, m2, m3, m4, m5, m6, m7))
    ms.core_start()
    ms.core_own()
    ms.y_start()
    ga_out[:, :H] = mm(gcf[...], kt[0], 1, 0).astype(BF16)
    ga_out[:, H:] = mm(gcf[...], kt[1], 1, 0).astype(BF16)
    cwf[rows(t, TB), :] = chunk_sum(cws, cwr, cw_in)
    cwg = TensorGather(lambda tt: cwf.at[rows(tt, TB), :])
    cwg.start()
    if MC == 0:
        cwg.mid()
    ms.z_start()
    if MC == 1:
        cwg.mid()
    step(1)
    mg = Gather(mt)

    def m_done():
        m_block = ms.z_end().astype(BF16)
        mt[c, yz_rows(y, z)] = m_block
        mch[c] = m_block
        mg.m_core = send(mch.at[c], mch.at[c], other)
        mg.start()

    if ZE == 0:
        m_done()
    mark()
    cwg.end()
    step(2)
    cwt[...] = cwf[...].T
    ds = Scatter(cwt, go, (d0, d1, d2, d3, d4, d5, d6, d7))
    ds.core_start()
    if ZE == 1:
        m_done()
    ds.core_own()
    ds.y_start()
    if ZE == 2:
        m_done()
    step(10)
    g_in = {}
    mg.m_core.wait_recv()
    for k in order + (0,):
        val = mm(mch[0], wv[t_to(k), :H, :], 1, 0) + mm(mch[1], wv[t_to(k), H:, :], 1, 0)
        if k:
            gs[k] = val.astype(BF16)
            g_in[k] = send(gs.at[k], gr.at[k], {"tensor": t_to(k)})
        else:
            gsum[...] = val
    flush()
    mg.z_step(1)
    mg.z_step(3)
    mg.z_step(2)
    mg.own_row()
    dec_out[...] = mm(cwf[...], dec[...], 1, 0).astype(BF16)
    step(3)
    ds.zc = {}
    ds.z_sum(2)
    for k in arrive:
        g_in[k].wait_recv()
        gsum[...] += gr[k].astype(F32)
    g_core = send(gsum.at[rows(1 - c, CB), :], gswp, other)
    mark()
    ds.z_sum(1)
    ds.z_sum(3)
    ds.z_sum(0)
    flush()
    mg.y_step(1)
    mg.y_step(3)
    mg.y_step(2)
    step(4)
    g_core.wait_recv()
    ge_out[:, me_h] = SCALE * gsum[rows(c, CB), :]
    ge_out[:, ot_h] = SCALE * gswp[...]
    dsum[...] = ds.z_end()
    d_core = send(dsum.at[rows(1 - c, CB), :], dswp, other)
    mg.finish()
    gw_out[:, :H] = SCALE * mm(erow[...], mt[0], 1, 0)
    gw_out[:, H:] = SCALE * mm(erow[...], mt[1], 1, 0)
    gd_out[:, me_h] = SCALE * dsum[rows(c, CB), :]
    d_core.wait_recv()
    gd_out[:, ot_h] = SCALE * dswp[...]

    for cp in sent:
        cp.wait_send()
    tree.drain()
    assert counter[0] <= N_COPIES, counter


def hand_on(*refs):
    copies = [pltpu.make_async_copy(refs[i], refs[5 + i], refs[10].at[i]) for i in range(5)]
    for cp in copies:
        cp.start()
    for cp in copies:
        cp.wait()


def scatter_scratch():
    v = pltpu.VMEM
    return [
        v((W, H), F32), v((W, H), BF16), v((W, H), BF16), v((3, YB, H), BF16), v((3, YB, H), BF16),
        v((3, ZB, H), BF16), v((3, ZB, H), BF16), v((ZB, H), F32),
    ]


def body(attended, out_weight, encoder, decoder, grad_out):
    v = pltpu.VMEM
    scratch = (
        [v((TOK, W), BF16), v((NT, W, H), BF16), v((H, W), BF16), v((W, W), BF16), v((TOK, W), BF16)]
        + [v((TOK, W), BF16), v((NT, TB, W), BF16), v((TOK, W), BF16), v((W, TOK), BF16)]
        + [v((NT, ZB, H), BF16), v((ZB, W), F32), v((ZB, H), BF16), v((ZB, H), BF16), v((2, W, H), BF16)]
        + scatter_scratch()
        + [v((2, ZB, H), BF16), v((2, W, H), BF16)]
        + [v((NT, ZB, H), BF16), v((NT, ZB, H), BF16), v((ZB, H), F32), v((CB, H), F32)]
        + [v((TOK, W), BF16), v((NT, TB, W), BF16), v((TOK, W), BF16), v((W, TOK), BF16)]
        + scatter_scratch()
        + [v((ZB, H), F32), v((CB, H), F32)]
        + [v((ER, W), BF16)]
        + [
            pltpu.SemaphoreType.DMA((20,)),
            pltpu.SemaphoreType.DMA((N_COPIES,)),
            pltpu.SemaphoreType.DMA((N_COPIES,)),
        ]
    )
    hbm = pl.BlockSpec(memory_space=pl.ANY)
    shapes = (
        jax.ShapeDtypeStruct((TOK, W), BF16),
        jax.ShapeDtypeStruct((TOK, W), BF16),
        jax.ShapeDtypeStruct((ER, W), F32),
        jax.ShapeDtypeStruct((CB, W), F32),
        jax.ShapeDtypeStruct((CB, W), F32),
    )
    results = pl.pallas_call(
        kernel,
        out_shape=tuple(pltpu.VMEM(a.shape, a.dtype) for a in shapes),
        in_specs=[hbm] * 5,
        out_specs=[pl.BlockSpec(memory_space=pltpu.VMEM)] * 5,
        scratch_shapes=scratch,
        compiler_params=pltpu.CompilerParams(
            collective_id=0, has_side_effects=True, vmem_limit_bytes=VMEM_LIMIT
        ),
    )(attended, out_weight, encoder, decoder, grad_out)
    decoded, grad_attended, weight_t, encoder_t, grad_decoder = pl.pallas_call(
        hand_on,
        out_shape=shapes,
        in_specs=[pl.BlockSpec(memory_space=pltpu.VMEM)] * 5,
        out_specs=[hbm] * 5,
        scratch_shapes=[pltpu.SemaphoreType.DMA((5,))],
        compiler_params=pltpu.CompilerParams(vmem_limit_bytes=32 * 1024 * 1024),
    )(*results)
    return decoded, grad_attended, weight_t.T, encoder_t.T, grad_decoder


def solution(mesh):
    return jax.shard_map(
        body,
        mesh=mesh,
        in_specs=(
            P("dp", "tensor"),
            P("tensor", None),
            P("tensor", None),
            P(None, "tensor"),
            P("dp", "tensor"),
        ),
        out_specs=(
            P("dp", "tensor"),
            P("dp", "tensor"),
            P("tensor", "dp"),
            P("tensor", "dp"),
            P("dp", "tensor"),
        ),
        check_vma=False,
    )
```

```python
import jax
import jax.numpy as jnp
from jax import lax
from jax.experimental import pallas as pl
from jax.experimental.pallas import tpu as pltpu
from jax.sharding import PartitionSpec as P

MESH = pl.DeviceIdType.MESH
F32 = jnp.float32
BF16 = jnp.bfloat16
TOK = 256
W = 768
H = W // 2
NY, NZ, NT = 4, 4, 8
YB = W // NY
ZB = YB // NZ
CB = ZB // 2
TB = TOK // NT
ER = W // 4
SCALE = 1.0 / float(8192) ** 0.5
N_COPIES = 140
VMEM_LIMIT = 60 * 1024 * 1024
T1 = 7
T2 = 2
T3 = 3
NO_TREE = False
TG = True
SORD = True
GCPOS = 2
GO = 1
ZE = 1
MC = 0
FL = True


def mm(a, b, ca, cb):
    return lax.dot_general(a, b, (((ca,), (cb,)), ((), ())), preferred_element_type=F32)


def kernel(
    att_h, w_h, enc_h, dec_h, go_h,
    dec_out, ga_out, gw_out, ge_out, gd_out,
    att, wv, enc, dec, go,
    gcs, gcr, gcf, gct,
    etr, kacc, ksnd, krcv, kt,
    m0, m1, m2, m3, m4, m5, m6, m7, mch, mt,
    gs, gr, gsum, gswp,
    cws, cwr, cwf, cwt,
    d0, d1, d2, d3, d4, d5, d6, d7, dsum, dswp,
    erow,
    lsem, ssem, rsem,
):
    d = lax.axis_index("dp")
    t = lax.axis_index("tensor")
    y, z, c = d // 8, (d // 2) % 4, d % 2
    zl, x = t // 4, t % 4
    sgn = 1 - 2 * c

    def dp_dev(yy, zz, cc):
        return {"dp": (yy % 4 * 4 + zz % 4) * 2 + cc}

    other = dp_dev(y, z, 1 - c)

    def y_dev(j):
        return dp_dev(y + j + 4, z, c)

    def z_dev(k):
        return dp_dev(y, z + k, c)

    def t_to(k):
        kz, kx = k // 4, k % 4
        return (1 - zl if kz else zl) * 4 + (x + kx) % 4

    def t_from(k):
        kz, kx = k // 4, k % 4
        return (1 - zl if kz else zl) * 4 + (x + 4 - kx) % 4

    order = (2, 6, 5, 7, 1, 3, 4)
    arrive = (1, 3, 4, 5, 7, 2, 6)

    def half(cc):
        return pl.ds(pl.multiple_of(cc * H, 128), H)

    def rows(i, n):
        return pl.ds(pl.multiple_of(i * n, n), n)

    me_h, ot_h = half(c), half(1 - c)

    def y_rows(yy):
        return rows((yy + 8) % 4, YB)

    def yz_rows(yy, zz):
        return rows((yy + 8) % 4 * 4 + (zz + 8) % 4, ZB)

    counter = [0]
    sent = []

    def remote(src, dst, dev):
        i = counter[0]
        counter[0] += 1
        cp = pltpu.make_async_remote_copy(
            src_ref=src, dst_ref=dst, send_sem=ssem.at[i], recv_sem=rsem.at[i],
            device_id=dev, device_id_type=MESH,
        )
        return cp

    def send(src, dst, dev):
        cp = remote(src, dst, dev)
        cp.start()
        sent.append(cp)
        return cp

    marks = []

    def mark():
        marks.append(len(sent))

    def flush():
        if FL:
            for cp in sent[: marks[-1]]:
                cp.wait_send()
            del sent[: marks[-1]]

    lcount = [0]

    def local(src, dst):
        i = lcount[0]
        lcount[0] += 1
        cp = pltpu.make_async_copy(src, dst, lsem.at[i])
        cp.start()
        return cp

    barrier = pltpu.get_barrier_semaphore()
    partners = (
        [{"tensor": t_to(k)} for k in order]
        + [y_dev(j) for j in (2, 1, 3)]
        + [z_dev(k) for k in (2, 1, 3)]
        + [other]
    )
    for dev in partners:
        pl.semaphore_signal(barrier, inc=1, device_id=dev, device_id_type=MESH)
    l_enc = local(enc_h.at[rows(c, H), :], enc)
    l_go = local(go_h, go)
    l_dec = local(dec_h, dec)

    l_enc.wait()
    pick = (
        lax.broadcasted_iota(jnp.int32, (ZB, W), 1)
        == lax.broadcasted_iota(jnp.int32, (ZB, W), 0) + (y * 4 + z) * ZB
    )
    pick = jnp.where(pick, 1.0, 0.0).astype(BF16)
    etr[t] = mm(pick, enc[...], 1, 1).astype(BF16)
    l_go.wait()
    l_dec.wait()
    l_w = []
    for i in range(NT):
        cols = pl.ds(pl.multiple_of(i * W + c * H, 128), H)
        l_w.append(local(w_h.at[:, cols], wv.at[i]))
    l_att = local(att_h, att)
    gcs[...] = mm(go[...], dec[...], 1, 1).astype(BF16)

    pl.semaphore_wait(barrier, len(partners))

    class TensorGather:
        def __init__(self, blk):
            self.blk = blk
            self.cp = {}

        def push(self, tt, k):
            self.cp[k] = send(self.blk(tt), self.blk(tt), {"tensor": t_to(k % 4 if TG else k)})

        def start(self):
            if not TG:
                for k in order:
                    self.push(t, k)
                return
            self.cp[4] = send(self.blk(t), self.blk(t), {"tensor": t_to(4)})
            for k in (2, 1, 3):
                self.push(t, k)

        def mid(self):
            if TG:
                self.cp[4].wait_recv()
                for k in (6, 5, 7):
                    self.push(t_to(4), k)

        def end(self, ks=arrive):
            for k in ks:
                if not (TG and k == 4):
                    self.cp[k].wait_recv()

    et = TensorGather(lambda tt: etr.at[tt])

    def gc_send():
        return {
            k: send(gcs.at[rows(t_to(k), TB), :], gcr.at[k], {"tensor": t_to(k)}) for k in order
        }

    et.start()
    if GCPOS == 0:
        gc_in = gc_send()
    et.mid()
    if GCPOS == 1:
        gc_in = gc_send()

    t_own = d // 4
    rx, rz = (x + 4 - t_own % 4) % 4, (zl + t_own // 4) % 2
    is_own = jnp.logical_and(rx == 0, rz == 0)
    is_two = jnp.logical_and(rx == 0, rz == 1)
    is_three = rx % 2 == 1
    is_last = rx == 2
    passes_on = rx == 1 + 2 * c
    e_recv = counter[0]
    counter[0] += 1
    e_send = [counter[0] + i for i in range(4)]
    counter[0] += 4

    def e_copy(i, dev):
        return pltpu.make_async_remote_copy(
            src_ref=erow, dst_ref=erow, send_sem=ssem.at[e_send[i]], recv_sem=rsem.at[e_recv],
            device_id={"tensor": dev}, device_id_type=MESH,
        )

    class Tree:
        def __init__(self):
            self.z = e_copy(0, (1 - zl) * 4 + x)
            self.p = e_copy(1, zl * 4 + (x + 1) % 4)
            self.m = e_copy(2, zl * 4 + (x + 3) % 4)
            self.f = e_copy(3, zl * 4 + (x + 4 + sgn) % 4)
            self.at = 0

        def step(self):
            self.at += 1
            if self.at == 1:

                @pl.when(is_own)
                def _():
                    cp = pltpu.make_async_copy(enc_h.at[rows(d % 4, ER), :], erow, lsem.at[19])
                    cp.start()
                    cp.wait()
                    self.z.start()
                    self.p.start()
                    self.m.start()

            elif self.at == 2:

                @pl.when(is_two)
                def _():
                    self.z.wait_recv()
                    self.p.start()
                    self.m.start()

            elif self.at == 3:

                @pl.when(is_three)
                def _():
                    self.z.wait_recv()

                @pl.when(passes_on)
                def _():
                    self.f.start()

            elif self.at == 4:

                @pl.when(is_last)
                def _():
                    self.z.wait_recv()

        def drain(self):
            if self.at == 0:
                return
            while self.at < 4:
                self.step()

            @pl.when(is_own)
            def _():
                self.z.wait_send()

            @pl.when(rx == 0)
            def _():
                self.p.wait_send()
                self.m.wait_send()

            @pl.when(passes_on)
            def _():
                self.f.wait_send()

    tree = Tree()

    def step(at):
        for i in (T1, T2, T3, 4):
            if i == at and not NO_TREE:
                tree.step()

    def chunk_sum(own, recv, copies):
        acc = own[rows(t, TB), :].astype(F32)
        for k in arrive:
            copies[k].wait_recv()
            acc = acc + recv[k].astype(F32)
        return acc.astype(BF16)

    gcg = TensorGather(lambda tt: gcf.at[rows(tt, TB), :])
    total = None
    for k in (0, 4, 1, 3, 2, 5, 7, 6):
        if k:
            et.end((k,))
        else:
            for cp in l_w:
                cp.wait()
        if k == 2 and GCPOS == 2:
            gc_in = gc_send()
        term = mm(etr[t_from(k)], wv[t_from(k)], 1, 1)
        total = term if total is None else total + term
    kacc[...] = total
    ksnd[...] = kacc[:, ot_h].astype(BF16)
    k_core = send(ksnd, krcv, other)
    if GCPOS == 3:
        gc_in = gc_send()

    class Gather:
        def __init__(self, buf):
            self.buf = buf
            self.yc = {}
            self.cc = []

        def push(self, r, dev):
            blk = self.buf.at[c, r]
            return send(blk, blk, dev)

        def y_send(self, k):
            for j in (2, 1, 3):
                self.yc[k, j] = self.push(yz_rows(y, z - k), y_dev(j))

        def start(self):
            self.zc = {k: self.push(yz_rows(y, z), z_dev(k)) for k in (2, 1, 3)}
            self.y_send(0)

        def z_step(self, k):
            self.zc[k].wait_recv()
            self.y_send(k)

        def z_rest(self):
            for k in (1, 3, 2):
                self.z_step(k)
            self.own_row()

        def own_row(self):
            self.cc.append(self.push(y_rows(y), other))

        def y_step(self, j):
            for k in (0, 1, 3, 2):
                self.yc[k, j].wait_recv()
            self.cc.append(self.push(y_rows(y - j), other))

        def y_rest(self):
            for j in (1, 3, 2):
                self.y_step(j)

        def finish(self):
            for cp in self.cc:
                cp.wait_recv()

    class Scatter:
        def __init__(self, lhs_t, right, bufs):
            self.lhs_t, self.right = lhs_t, right
            self.own, self.oth, self.rcv, self.ys, self.yr, self.zs, self.zr, self.zown = bufs

        def core_start(self):
            self.cc = {}
            for j in (2, 1, 3, 0):
                r = y_rows(y + j)
                self.oth[r, :] = mm(self.lhs_t[r, :], self.right[:, ot_h], 1, 0).astype(BF16)
                self.cc[j] = send(self.oth.at[r, :], self.rcv.at[r, :], other)

        def core_own(self):
            for j in (2, 1, 3, 0):
                r = y_rows(y + j)
                self.own[r, :] = mm(self.lhs_t[r, :], self.right[:, me_h], 1, 0)

        def y_send(self, k, j):
            r = rows((z + k) % 4, ZB)
            self.yc[k, j] = send(self.ys.at[j - 1, r, :], self.yr.at[j - 1, r, :], y_dev(j))

        def y_start(self):
            self.yc = {}
            for j in (2, 1, 3):
                r = y_rows(y + j)
                self.cc[j].wait_recv()
                self.ys[j - 1] = (self.own[r, :] + self.rcv[r, :].astype(F32)).astype(BF16)
                if SORD and j == 2:
                    for k in (2, 1, 3, 0):
                        self.y_send(k, j)
            for k in (2, 1, 3, 0):
                for j in (1, 3) if SORD else (2, 1, 3):
                    self.y_send(k, j)
            self.cc[0].wait_recv()

        def z_start(self):
            self.zc = {}
            for k in (2, 1, 3, 0):
                self.z_sum(k)

        def z_sum(self, k):
            if 1:
                r = rows((z + k) % 4, ZB)
                yz = yz_rows(y, z + k)
                val = self.own[yz, :] + self.rcv[yz, :].astype(F32)
                for j in (1, 3, 2):
                    self.yc[k, j].wait_recv()
                    val = val + self.yr[j - 1, r, :].astype(F32)
                if k:
                    self.zs[k - 1] = val.astype(BF16)
                    self.zc[k] = send(self.zs.at[k - 1], self.zr.at[k - 1], z_dev(k))
                else:
                    self.zown[...] = val

        def z_end(self):
            val = self.zown[...]
            for k in (1, 3, 2):
                self.zc[k].wait_recv()
                val = val + self.zr[k - 1].astype(F32)
            return val

    k_core.wait_recv()
    kt[c, yz_rows(y, z)] = (kacc[:, me_h] + krcv[...].astype(F32)).astype(BF16)
    kg = Gather(kt)
    kg.start()
    if GO == 1:
        gcf[rows(t, TB), :] = chunk_sum(gcs, gcr, gc_in)
        gcg.start()
        kg.z_step(1)
        kg.z_step(3)
        gcg.mid()
        kg.z_step(2)
        kg.own_row()
    else:
        kg.z_step(1)
        kg.z_step(3)
        kg.z_step(2)
        kg.own_row()
        gcf[rows(t, TB), :] = chunk_sum(gcs, gcr, gc_in)
        gcg.start()
        gcg.mid()
    step(7)

    kg.y_step(1)
    kg.y_step(3)
    kg.y_step(2)
    kg.finish()

    l_att.wait()
    cw_in = {}
    for side, ks in ((1 - zl, (6, 5, 7, 4)), (zl, (2, 1, 3))):
        r = rows(side, TOK // 2)
        cws[r, :] = (mm(att[r, :H], kt[0], 1, 1) + mm(att[r, H:], kt[1], 1, 1)).astype(BF16)
        for k in ks:
            cw_in[k] = send(cws.at[rows(t_to(k), TB), :], cwr.at[k], {"tensor": t_to(k)})
    gcg.end()
    step(9)
    gct[...] = gcf[...].T
    ms = Scatter(gct, att, (m0, m1, m2, m3, m4, m5, m6, m7))
    ms.core_start()
    ms.core_own()
    ms.y_start()
    ga_out[:, :H] = mm(gcf[...], kt[0], 1, 0).astype(BF16)
    ga_out[:, H:] = mm(gcf[...], kt[1], 1, 0).astype(BF16)
    cwf[rows(t, TB), :] = chunk_sum(cws, cwr, cw_in)
    cwg = TensorGather(lambda tt: cwf.at[rows(tt, TB), :])
    cwg.start()
    if MC == 0:
        cwg.mid()
    ms.z_start()
    if MC == 1:
        cwg.mid()
    step(1)
    mg = Gather(mt)

    def m_done():
        m_block = ms.z_end().astype(BF16)
        mt[c, yz_rows(y, z)] = m_block
        mch[c] = m_block
        mg.m_core = send(mch.at[c], mch.at[c], other)
        mg.start()

    if ZE == 0:
        m_done()
    mark()
    cwg.end()
    step(2)
    cwt[...] = cwf[...].T
    ds = Scatter(cwt, go, (d0, d1, d2, d3, d4, d5, d6, d7))
    ds.core_start()
    if ZE == 1:
        m_done()
    ds.core_own()
    ds.y_start()
    if ZE == 2:
        m_done()
    step(10)
    g_in = {}
    mg.m_core.wait_recv()
    for k in order + (0,):
        val = mm(mch[0], wv[t_to(k), :H, :], 1, 0) + mm(mch[1], wv[t_to(k), H:, :], 1, 0)
        if k:
            gs[k] = val.astype(BF16)
            g_in[k] = send(gs.at[k], gr.at[k], {"tensor": t_to(k)})
        else:
            gsum[...] = val
    flush()
    mg.z_step(1)
    mg.z_step(3)
    mg.z_step(2)
    mg.own_row()
    dec_out[...] = mm(cwf[...], dec[...], 1, 0).astype(BF16)
    step(3)
    ds.zc = {}
    ds.z_sum(2)
    for k in arrive:
        g_in[k].wait_recv()
        gsum[...] += gr[k].astype(F32)
    g_core = send(gsum.at[rows(1 - c, CB), :], gswp, other)
    mark()
    ds.z_sum(1)
    ds.z_sum(3)
    ds.z_sum(0)
    flush()
    mg.y_step(1)
    mg.y_step(3)
    mg.y_step(2)
    step(4)
    g_core.wait_recv()
    ge_out[:, me_h] = SCALE * gsum[rows(c, CB), :]
    ge_out[:, ot_h] = SCALE * gswp[...]
    dsum[...] = ds.z_end()
    d_core = send(dsum.at[rows(1 - c, CB), :], dswp, other)
    mg.finish()
    gw_out[:, :H] = SCALE * mm(erow[...], mt[0], 1, 0)
    gw_out[:, H:] = SCALE * mm(erow[...], mt[1], 1, 0)
    gd_out[:, me_h] = SCALE * dsum[rows(c, CB), :]
    d_core.wait_recv()
    gd_out[:, ot_h] = SCALE * dswp[...]

    for cp in sent:
        cp.wait_send()
    tree.drain()
    assert counter[0] <= N_COPIES, counter


def hand_on(*refs):
    copies = [pltpu.make_async_copy(refs[i], refs[5 + i], refs[10].at[i]) for i in range(5)]
    for cp in copies:
        cp.start()
    for cp in copies:
        cp.wait()


def scatter_scratch():
    v = pltpu.VMEM
    return [
        v((W, H), F32), v((W, H), BF16), v((W, H), BF16), v((3, YB, H), BF16), v((3, YB, H), BF16),
        v((3, ZB, H), BF16), v((3, ZB, H), BF16), v((ZB, H), F32),
    ]


def body(attended, out_weight, encoder, decoder, grad_out):
    v = pltpu.VMEM
    scratch = (
        [v((TOK, W), BF16), v((NT, W, H), BF16), v((H, W), BF16), v((W, W), BF16), v((TOK, W), BF16)]
        + [v((TOK, W), BF16), v((NT, TB, W), BF16), v((TOK, W), BF16), v((W, TOK), BF16)]
        + [v((NT, ZB, H), BF16), v((ZB, W), F32), v((ZB, H), BF16), v((ZB, H), BF16), v((2, W, H), BF16)]
        + scatter_scratch()
        + [v((2, ZB, H), BF16), v((2, W, H), BF16)]
        + [v((NT, ZB, H), BF16), v((NT, ZB, H), BF16), v((ZB, H), F32), v((CB, H), F32)]
        + [v((TOK, W), BF16), v((NT, TB, W), BF16), v((TOK, W), BF16), v((W, TOK), BF16)]
        + scatter_scratch()
        + [v((ZB, H), F32), v((CB, H), F32)]
        + [v((ER, W), BF16)]
        + [
            pltpu.SemaphoreType.DMA((20,)),
            pltpu.SemaphoreType.DMA((N_COPIES,)),
            pltpu.SemaphoreType.DMA((N_COPIES,)),
        ]
    )
    hbm = pl.BlockSpec(memory_space=pl.ANY)
    shapes = (
        jax.ShapeDtypeStruct((TOK, W), BF16),
        jax.ShapeDtypeStruct((TOK, W), BF16),
        jax.ShapeDtypeStruct((ER, W), F32),
        jax.ShapeDtypeStruct((CB, W), F32),
        jax.ShapeDtypeStruct((CB, W), F32),
    )
    results = pl.pallas_call(
        kernel,
        out_shape=tuple(pltpu.VMEM(a.shape, a.dtype) for a in shapes),
        in_specs=[hbm] * 5,
        out_specs=[pl.BlockSpec(memory_space=pltpu.VMEM)] * 5,
        scratch_shapes=scratch,
        compiler_params=pltpu.CompilerParams(
            collective_id=0, has_side_effects=True, vmem_limit_bytes=VMEM_LIMIT
        ),
    )(attended, out_weight, encoder, decoder, grad_out)
    decoded, grad_attended, weight_t, encoder_t, grad_decoder = pl.pallas_call(
        hand_on,
        out_shape=shapes,
        in_specs=[pl.BlockSpec(memory_space=pltpu.VMEM)] * 5,
        out_specs=[hbm] * 5,
        scratch_shapes=[pltpu.SemaphoreType.DMA((5,))],
        compiler_params=pltpu.CompilerParams(vmem_limit_bytes=32 * 1024 * 1024),
    )(*results)
    return decoded, grad_attended, weight_t.T, encoder_t.T, grad_decoder


def solution(mesh):
    return jax.shard_map(
        body,
        mesh=mesh,
        in_specs=(
            P("dp", "tensor"),
            P("tensor", None),
            P("tensor", None),
            P(None, "tensor"),
            P("dp", "tensor"),
        ),
        out_specs=(
            P("dp", "tensor"),
            P("dp", "tensor"),
            P("tensor", "dp"),
            P("tensor", "dp"),
            P("dp", "tensor"),
        ),
        check_vma=False,
    )
```
